256 devices in a mesh: pos: 128 (over y, z, x), pix: 2 (over core).
Axes of the slice: x: 4, y: 4, z: 8, core: 2. Of those that a mesh axis runs over, the one named last changes fastest.
Arguments:
- frames: float32 [8192, 128, 128], P('pos', None, 'pix'), may hold values from -96 to 96
- sketch: bfloat16 [128, 128, 256], P(None, 'pix'), may hold values from -0.046875 to 0.046875
Outputs:
- denoised: float32 [128, 128, 8192], P('pos', 'pix')
The draws below stay inside these ranges and needn't reach their ends.
All inputs are finite; a program needn't handle non-finite values.
Results may differ from the reference program's by a relative error of at most 0.0037.
Values sent between devices are 32-bit elements; how exact they have to be, the bound alone decides.
A program may use at most 128 MiB of HBM per device.

```python
import jax
import jax.numpy as jnp
from jax import lax

DET_ROWS = 128
DET_COLS = 128
RANK = 256
FRAMES = 8192


def raised(entries, rng, source, target, blocks, factor):
    owner, partner = [(jnp.arange(entries.shape[axis_at]) // (entries.shape[axis_at] // blocks)).reshape([-1 if axis == axis_at else 1 for axis in range(entries.ndim)]) for axis_at in (source, target)]
    chosen = jax.random.permutation(rng, blocks)[partner]
    strong = (owner == chosen) | (owner == (partner + blocks // 2) % blocks)
    return jnp.where(strong, factor * entries, entries)


def levels(key, dims, split, least, largest):
    loudness = 1.0
    for axis_at, shards_of in split:
        draws = jax.random.uniform(jax.random.fold_in(jax.random.fold_in(key, 6), axis_at), (shards_of,), jnp.float32, least / len(split), largest / len(split))
        loudness = loudness * jnp.repeat(jnp.exp(draws), dims[axis_at] // shards_of).reshape((-1,) + (1,) * (len(dims) - 1 - axis_at))
    return loudness


def noise(stream_key, extent, scale, most, cuts=(), kind=jnp.bfloat16):
    gain = levels(stream_key, extent, cuts, -0.22, 0.18) if cuts else 1.0
    values = jax.random.normal(stream_key, extent, jnp.float32) * scale * gain
    return jnp.minimum(jnp.maximum(values, -most), most).astype(kind)


def gaussian_with(key, dims, deviation, bound, split, heavy, dtype=jnp.bfloat16):
    entries = deviation * jax.random.normal(key, dims, jnp.float32)
    if split:
        entries = entries * levels(key, dims, split, -0.22, 0.18)
    return jnp.clip(raised(entries, jax.random.fold_in(key, 3), *heavy), -bound, bound).astype(dtype)


def setup_inputs(seed: int = 0) -> dict:
    keys = jax.random.split(jax.random.key(seed), 3)
    return {
        "frames": gaussian_with(keys[0], (FRAMES, DET_ROWS, DET_COLS), 4.0, 96.0, ((0, 128), (2, 2)), (0, 1, 128, 5.5), jnp.float32),
        "sketch": noise(keys[1], (DET_ROWS, DET_COLS, RANK), (DET_ROWS * DET_COLS) ** -0.5, 0.046875, ((1, 2),)),
    }


def reference(frames, sketch):
    whole = frames.reshape(FRAMES, DET_ROWS * DET_COLS)
    test_matrix = sketch.reshape(DET_ROWS * DET_COLS, RANK)
    sketched = jnp.dot(whole.astype(jnp.bfloat16).astype(jnp.float32), test_matrix.astype(jnp.float32), preferred_element_type=jnp.float32)
    gram = jnp.dot(sketched.T.astype(jnp.float32), sketched.astype(jnp.float32), precision=lax.Precision.HIGHEST, preferred_element_type=jnp.float32)
    factor = jnp.linalg.cholesky(gram)
    basis_t = lax.linalg.triangular_solve(factor, sketched.T, left_side=True, lower=True)
    coeffs = jnp.dot(whole.T.astype(jnp.float32), basis_t.T.astype(jnp.float32), precision=lax.Precision.HIGHEST, preferred_element_type=jnp.float32)
    rebuilt = jnp.dot(coeffs.astype(jnp.float32), basis_t.astype(jnp.float32), precision=lax.Precision.HIGHEST, preferred_element_type=jnp.float32)
    return rebuilt.reshape(DET_ROWS, DET_COLS, FRAMES)
```

```python
import jax
import jax.numpy as jnp
from jax import lax
from jax.experimental import pallas as pl
from jax.experimental.pallas import tpu as pltpu
from jax.sharding import PartitionSpec as P

MESH = pl.DeviceIdType.MESH
HIGHEST = lax.Precision.HIGHEST
NY, NZ, NX = 4, 8, 4
PLANE = NY * NX
RANK = 256
BLOCK, PANEL = 8, 32
TIES = [k for k in range(1, PLANE) if k // NX == 2 or k % NX == 2]
EARLY = [1, 3]
LATE = [k for k in range(1, PLANE) if k not in TIES + EARLY]


def tn(a, b, precision=None):
    return lax.dot_general(a, b, (((0,), (0,)), ((), ())), precision=precision, preferred_element_type=jnp.float32)


def nt(a, b, precision=None):
    return lax.dot_general(a, b, (((1,), (1,)), ((), ())), precision=precision, preferred_element_type=jnp.float32)


def nn(a, b, precision=None):
    return jnp.dot(a, b, precision=precision, preferred_element_type=jnp.float32)


def halves(a):
    high = a.astype(jnp.bfloat16)
    return high, (a - high.astype(jnp.float32)).astype(jnp.bfloat16)


def splat(rows, i):
    return jnp.broadcast_to(rows[:, i : i + 1], (BLOCK, 128))


def lanes_of(rows, base):
    tile = jnp.where(base < 128, rows[:, 0:128], rows[:, 128:256])
    return pltpu.roll(tile, lax.rem(256 - base, 128), 1)


def factor_diagonal(a):
    groups = [a[g * BLOCK : (g + 1) * BLOCK] for g in range(PANEL // BLOCK)]
    sub = lax.broadcasted_iota(jnp.int32, (BLOCK, 128), 0)
    for q in range(PANEL // BLOCK):
        rows = [jnp.broadcast_to(groups[q][k : k + 1, :], (BLOCK, 128)) for k in range(BLOCK)]
        columns = [[splat(groups[g], q * BLOCK + k) for k in range(BLOCK)] for g in range(q + 1, PANEL // BLOCK)]
        s = [[splat(rows[i], q * BLOCK + k) for k in range(i + 1)] for i in range(BLOCK)]
        inv, done = [], []
        for k in range(BLOCK):
            inv.append(lax.rsqrt(s[k][k]))
            for i in range(k + 1, BLOCK):
                s[i][k] = s[i][k] * inv[k]
            for i in range(k + 1, BLOCK):
                for m in range(k + 1, i + 1):
                    s[i][m] = s[i][m] - s[i][k] * s[m][k]
            row = rows[k]
            for i in range(k):
                row = row - s[k][i] * done[i]
            done.append(row * inv[k])
        for g in range(q + 1, PANEL // BLOCK):
            times = []
            for k in range(BLOCK):
                t = columns[g - q - 1][k]
                for i in range(k):
                    t = t - times[i] * s[k][i]
                times.append(t * inv[k])
                groups[g] = groups[g] - times[k] * done[k]
        block = done[0]
        for k in range(1, BLOCK):
            block = jnp.where(sub == k, done[k], block)
        groups[q] = block
    return jnp.concatenate(groups, axis=0)


def factor_step(o, last, a_ref):
    base = pl.multiple_of(o * PANEL, PANEL)
    lane = lax.broadcasted_iota(jnp.int32, (1, RANK), 1)
    before = (lane >= base - PANEL) & (lane < base)
    rows = jnp.where(before, 0.0, a_ref[pl.ds(base, PANEL), :])
    rows = rows - tn(lanes_of(last, base)[:, 0:PANEL], last, HIGHEST)
    row_at = lax.broadcasted_iota(jnp.int32, (PANEL, 128), 0)
    lane_at = lax.broadcasted_iota(jnp.int32, (PANEL, 128), 1)
    both = jnp.where(lane_at < PANEL, lanes_of(rows, base), jnp.where(lane_at == row_at + PANEL, 1.0, 0.0))
    both = factor_diagonal(both)
    inverse = jnp.where((lane_at >= PANEL) & (lane_at < 2 * PANEL), both, 0.0)
    own = (lane >= base) & (lane < base + PANEL)
    unit = lane == base + lax.broadcasted_iota(jnp.int32, (PANEL, 1), 0)
    rows = jnp.where(own, jnp.where(unit, 1.0, 0.0), rows)
    zeros = jnp.zeros((PANEL, RANK), jnp.float32)
    panel = nn(inverse, jnp.concatenate([zeros, rows, zeros, zeros], axis=0), HIGHEST)
    right = jnp.where(lane >= base, last, 0.0)
    below = lax.broadcasted_iota(jnp.int32, (RANK, 1), 0) >= base
    a_ref[...] = jnp.where(below & before, 0.0, a_ref[...]) - tn(right, last, HIGHEST)

    @pl.when(o > 0)
    def _():
        a_ref[pl.ds(pl.multiple_of(jnp.maximum(base - PANEL, 0), PANEL), PANEL), :] = last

    return panel


def main_kernel(
    x_hbm, s_hbm, w_ref, ya,
    xv, xt, sv, msg, xr, part, other, yl, yp, gl, gr, gp, gz, gf, gm, cacc, cr, vb, gi,
    x_in, s_in, pair_send, pair_recv, x_send, x_recv, y_send, y_recv, half_send, half_recv, own_sem,
    g_send, g_recv, gz_send, gz_recv, gf_send, gf_recv, c_send, c_recv,
    up_send, up_recv, down_send, down_recv, zd_send, zd_recv, p1_send, p1_recv, p2_send, p2_recv, fwd_send, fwd_recv,
    via_send, via_recv, on_send, gi_send, gi_recv,
):
    me = lax.axis_index("pos")
    core = lax.axis_index("pix")
    my_y, my_z, my_x = me // (NZ * NX), (me // NX) % NZ, me % NX
    my_d = my_y * NX + my_x
    sibling = 1 - core

    def at(y, z, x):
        return y * (NZ * NX) + z * NX + x

    def at_d(d):
        return at(d // NX, my_z, d % NX)

    def other_d(k):
        return lax.rem(my_y + k // NX, NY) * NX + lax.rem(my_x + k % NX, NX)

    def other_z(k):
        return lax.rem(my_z + k, NZ)

    def remote(src, dst, send_sem, recv_sem, pos, to_core):
        return pltpu.make_async_remote_copy(
            src_ref=src, dst_ref=dst, send_sem=send_sem, recv_sem=recv_sem,
            device_id={"pos": pos, "pix": to_core}, device_id_type=MESH,
        )

    def landed(ref, sem):
        remote(ref, ref, own_sem.at[0], sem, me, sibling).wait_recv()

    def left(ref, sem):
        remote(ref, ref, sem, own_sem.at[0], me, sibling).wait_send()

    x_copy_in = pltpu.make_async_copy(x_hbm, xv, x_in)
    x_copy_in.start()
    s_copy_in = pltpu.make_async_copy(s_hbm, sv, s_in)
    s_copy_in.start()

    barrier = pltpu.get_barrier_semaphore()

    def greet(pos, to_core):
        pl.semaphore_signal(barrier, inc=1, device_id={"pos": pos, "pix": to_core}, device_id_type=MESH)

    greet(me, sibling)

    @pl.loop(1, PLANE)
    def _(k):
        greet(at_d(other_d(k)), core)
        greet(at_d(other_d(k)), sibling)

    @pl.loop(1, NZ)
    def _(k):
        greet(at(my_y, other_z(k), my_x), core)

    x_copy_in.wait()

    @pl.loop(0, 32, unroll=4)
    def _(cp):
        low = xv[pl.ds(cp, 64, stride=64), :]
        high = xv[pl.ds(cp + 32, 64, stride=64), :]
        xt[pl.ds(pl.multiple_of(cp * 128, 128), 128), :] = jnp.concatenate([low, high], axis=0).T

    s_copy_in.wait()
    pl.semaphore_wait(barrier, 1 + 2 * (PLANE - 1) + NZ - 1)

    def x_copy(k, wave):
        d = other_d(k)
        if k in TIES:
            rows = pl.ds(0, 3) if wave == 0 else pl.ds(7, 1)
        else:
            rows = pl.ds(0, 5) if wave == 0 else pl.ds(5, 3)
        return remote(msg.at[d, rows], xr.at[my_d, rows], x_send, x_recv.at[wave], at_d(d), core)

    def via(k):
        return 3 if k // NX == 2 else k // NX, 3 if k % NX == 2 else k % NX

    def via_copy(n):
        k = TIES[n]
        vy, vx = via(k)
        pos = at(lax.rem(my_y + vy, NY), my_z, lax.rem(my_x + vx, NX))
        return remote(msg.at[other_d(k), pl.ds(3, 4)], vb.at[n], via_send, via_recv.at[n], pos, core)

    def on_copy(n, wave):
        k = TIES[n]
        vy, vx = via(k)
        from_d = lax.rem(my_y + NY - vy, NY) * NX + lax.rem(my_x + NX - vx, NX)
        pos = at(lax.rem(my_y + NY + k // NX - vy, NY), my_z, lax.rem(my_x + NX + k % NX - vx, NX))
        src, dst = vb.at[n, pl.ds(2 * wave, 2)], xr.at[from_d, pl.ds(3 + 2 * wave, 2)]
        return remote(src, dst, on_send, x_recv.at[wave], pos, core)

    total = jnp.zeros((64, RANK), jnp.float32)
    for k in TIES + EARLY + LATE + [0]:
        d = other_d(k)
        rows = [xt[pl.ds(at(d // NX, zz, d % NX), 32, stride=128), :] for zz in range(NZ)]
        for zz in range(NZ):
            msg[d, pl.ds(lax.rem(zz + 2 * NZ - 2 - my_z, NZ), 1)] = rows[zz].reshape(1, 32, 128)
        if k in TIES:
            via_copy(TIES.index(k)).start()
        if k in EARLY:
            x_copy(k, 0).start()
            x_copy(k, 1).start()
        xb = jnp.concatenate(rows, axis=0).T.astype(jnp.bfloat16)
        low = sv[d // NX, :, d % NX, 0:32, :].reshape(256, RANK)
        high = sv[d // NX, :, d % NX, 32:64, :].reshape(256, RANK)
        total = total + nn(xb[0:64], low) + nn(xb[64:128], high)
    part[...] = total
    pair = remote(part, other, pair_send, pair_recv, me, sibling)
    pair.start()
    xr[pl.ds(my_d, 1)] = msg[pl.ds(my_d, 1)]
    pair.wait()
    yl[...] = part[...] + other[...]
    my_half = pl.ds(pl.multiple_of(core * 32, 32), 32)
    yp[pl.ds(core, 1), pl.ds(my_d, 1)] = yl[my_half, :].reshape(1, 1, 32, RANK)
    gl[...] = tn(yl[...], yl[...], HIGHEST)

    def g_copy(k):
        d = other_d(k)
        rows = pl.ds(pl.multiple_of(core * 128 + d * 8, 8), 8)
        return remote(gl.at[rows, :], gr.at[my_d], g_send, g_recv, at_d(d), core)

    def gz_copy(k):
        z = other_z(k)
        return remote(gp, gz.at[my_z], gz_send, gz_recv, at(my_y, z, my_x), core)

    my_rows = pl.ds(pl.multiple_of((core * PLANE + my_d) * 8, 8), 8)

    def gf_copy(d, q):
        return remote(gf, gm.at[my_rows, :], gf_send, gf_recv, at_d(d), q)

    def y_copy(k):
        d = other_d(k)
        return remote(yl.at[my_half, :], yp.at[core, my_d], y_send, y_recv, at_d(d), core)

    half_copy = remote(yp.at[core], yp.at[core], half_send, half_recv, me, sibling)

    def own_copy(q):
        return pltpu.make_async_copy(yp.at[q], ya.at[0, q], own_sem.at[q])

    above, below = at(my_y, other_z(1), my_x), at(my_y, other_z(NZ - 1), my_x)

    def up_copy(r):
        src = yp.at[0] if r == 0 else ya.at[NZ - r, 0]
        dst = ya.at[NZ - 1 - r, 0]
        if r == 3:
            src, dst = src.at[pl.ds(0, 8)], dst.at[pl.ds(0, 8)]
        return remote(src, dst, up_send.at[r], up_recv.at[r], above, 0)

    def down_copy(r):
        src = yp.at[0] if r == 0 else ya.at[r, 0]
        dst = ya.at[1 + r, 0]
        if r == 3:
            src, dst = src.at[pl.ds(8, 8)], dst.at[pl.ds(8, 8)]
        return remote(src, dst, down_send.at[r], down_recv.at[r], below, 0)

    def forward(ref):
        remote(ref, ref, fwd_send, fwd_recv, me, sibling).start()

    def zd_copy(k):
        return remote(
            yl.at[my_half, :], ya.at[NZ - k, 1, my_d], zd_send, zd_recv, at(my_y, other_z(k), my_x), 1
        )

    near, far = pl.ds(1, 4), pl.ds(5, 3)

    upper, lower = pl.ds(0, 16), pl.ds(16, 16)

    def x_next(i):
        return lax.rem(my_x + i, NX)

    def y_next(i):
        return lax.rem(my_y + i, NY)

    def p1_copies(t):
        copies = []
        for q, (rel, block, along) in enumerate((
            (near, lambda i: my_y * NX + x_next(i), lambda i: at(my_y, my_z, x_next(i))),
            (far, lambda i: y_next(i) * NX + my_x, lambda i: at(y_next(i), my_z, my_x)),
        )):
            if t == 0:
                up, down = ya.at[rel, 1, block(0)], ya.at[rel, 1, block(0)]
            else:
                up, down = ya.at[rel, 1, block(3), upper], ya.at[rel, 1, block(1), lower]
            copies.append(remote(up, up, p1_send.at[t, q], p1_recv.at[t, q], along(1), 1))
            copies.append(remote(down, down, p1_send.at[t, q], p1_recv.at[t, q], along(3), 1))
        return copies

    def p2_copies(t):
        def row(i):
            return pl.ds(pl.multiple_of(y_next(i) * NX, NX), NX)

        copies = []
        if t == 0:
            up, down = ya.at[near, 1, row(0)], ya.at[near, 1, row(0)]
        else:
            up, down = ya.at[near, 1, row(3), upper], ya.at[near, 1, row(1), lower]
        copies.append(remote(up, up, p2_send.at[t, 0], p2_recv.at[t, 0], at(y_next(1), my_z, my_x), 1))
        copies.append(remote(down, down, p2_send.at[t, 0], p2_recv.at[t, 0], at(y_next(3), my_z, my_x), 1))
        for v in range(NY):
            if t == 0:
                up, down = ya.at[far, 1, v * NX + my_x], ya.at[far, 1, v * NX + my_x]
            else:
                up, down = ya.at[far, 1, v * NX + x_next(3), upper], ya.at[far, 1, v * NX + x_next(1), lower]
            copies.append(remote(up, up, p2_send.at[t, 1], p2_recv.at[t, 1], at(my_y, my_z, x_next(1)), 1))
            copies.append(remote(down, down, p2_send.at[t, 1], p2_recv.at[t, 1], at(my_y, my_z, x_next(3)), 1))
        return copies

    def p_forward(i):
        forward(ya.at[near, 1, pl.ds(pl.multiple_of(y_next(i) * NX, NX), NX)])
        for v in range(NY):
            forward(ya.at[far, 1, v * NX + x_next(i)])

    def p_size(phase, t):
        blocks = (1 if phase == 1 else 4) * (2 if t == 0 else 1)
        return [ya.at[near, 1, pl.ds(0, blocks)], ya.at[far, 1, pl.ds(0, blocks)]]

    def p_landed(phase, t):
        for q in range(2):
            landed(p_size(phase, t)[q], (p1_recv if phase == 1 else p2_recv).at[t, q])

    def p_start(phase, t):
        for copy in (p1_copies if phase == 1 else p2_copies)(t):
            copy.start()

    @pl.loop(1, PLANE)
    def _(k):
        g_copy(k).start()

    @pl.loop(1, PLANE)
    def _(k):
        y_copy(k).start()

    gr[pl.ds(my_d, 1)] = gl[my_rows, :].reshape(1, 8, RANK)

    @pl.when(core == 1)
    def _():
        @pl.loop(1, NZ)
        def _(k):
            zd_copy(k).start()

    landed(gr.at[pl.ds(0, PLANE - 1)], g_recv)
    gp[...] = jnp.sum(gr[...], axis=0)

    @pl.loop(1, NZ)
    def _(k):
        gz_copy(k).start()

    gz[pl.ds(my_z, 1)] = gp[...].reshape(1, 8, RANK)
    landed(gz.at[pl.ds(0, NZ - 1)], gz_recv)
    gf[...] = jnp.sum(gz[...], axis=0)

    @pl.when(core == 0)
    def _():
        gf_copy(my_d, 1).start()

    @pl.loop(1, PLANE)
    def _(k):
        gf_copy(other_d(k), 1).start()

    gm[my_rows, :] = gf[...]
    landed(yp.at[core, pl.ds(0, PLANE - 1)], y_recv)
    half_copy.start()
    own_copy(core).start()

    @pl.when(core == 0)
    def _():
        up_copy(0).start()
        down_copy(0).start()

    @pl.when(core == 1)
    def _():
        landed(ya.at[pl.ds(1, NZ - 1), 1, my_d], zd_recv)
        p_start(1, 0)

    def frames_on(wave):
        for k in LATE:
            x_copy(k, wave).start()
        for n in range(len(TIES)):
            if wave == 0:
                landed(vb.at[n], via_recv.at[n])
            on_copy(n, wave).start()
        for k in TIES:
            x_copy(k, wave).start()

    def ring_landed(r):
        if r < 3:
            landed(ya.at[NZ - 1 - r, 0], up_recv.at[r])
            landed(ya.at[1 + r, 0], down_recv.at[r])
        else:
            landed(ya.at[4, 0, pl.ds(0, 8)], up_recv.at[r])
            landed(ya.at[4, 0, pl.ds(8, 8)], down_recv.at[r])

    def ring_round(r):
        ring_landed(r - 1)
        up_copy(r).start()
        down_copy(r).start()
        forward(ya.at[NZ - r, 0])
        forward(ya.at[r, 0])

    def c_block(s, way):
        return pl.ds((2 - s if way == 0 else 2 + s) % NZ if s < 3 else (7 if way == 0 else 5), 1)

    def c_rows(s, way):
        return pl.ds(0, 32) if s else pl.ds(16 * way, 16)

    def c_copy(s, way):
        src, dst = cacc.at[c_block(s, way), c_rows(s, way)], cr.at[way, pl.ds(s, 1), c_rows(s, way)]
        return remote(src, dst, c_send.at[way, s], c_recv.at[way, s], above if way == 0 else below, core)

    def c_landed(s, way):
        landed(cr.at[way, pl.ds(s, 1), c_rows(s, way)], c_recv.at[way, s])

    def c_step(s):
        for way in range(2):
            if s:
                c_landed(s - 1, way)
                rows = c_rows(s - 1, way)
                cacc[c_block(s, way), rows] += cr[way, pl.ds(s - 1, 1), rows]
            c_copy(s, way).start()

    def coefficients(rows):
        ks = range(PLANE)
        total = jnp.zeros((rows.size * 32, 2 * RANK), jnp.float32)
        zero = jnp.zeros((64, RANK), jnp.float32)
        for n in range(0, len(ks), 2):
            lhs, rhs = [], []
            for k in ks[n : n + 2]:
                d = other_d(k)
                y = jnp.concatenate([yp[0, d], yp[1, d]], axis=0)
                lhs.append(xr[d, rows].reshape(rows.size * 32, 128))
                rhs.append(jnp.concatenate([y, zero], axis=1))
                rhs.append(jnp.concatenate([zero, y], axis=1))
            ah, al = halves(jnp.concatenate(lhs, axis=1))
            bh, bl = halves(jnp.concatenate(rhs, axis=0))
            total = total + (nn(ah, bh) + nn(ah, bl) + nn(al, bh))
        cacc[rows] = total.reshape(rows.size, 32, 2 * RANK)

    def first_sums():
        landed(yp.at[sibling], half_recv)
        own_copy(sibling).start()
        landed(xr.at[pl.ds(0, PLANE - 1), pl.ds(0, 5)], x_recv.at[0])
        coefficients(pl.ds(0, 5))
        c_step(0)

    def second_sums():
        landed(xr.at[pl.ds(0, PLANE - 1), pl.ds(0, 3)], x_recv.at[1])
        coefficients(pl.ds(5, 3))
        c_step(3)

    def step(o, last):
        @pl.when(o == 1)
        def _():
            p_landed(1, 1)
            p_start(2, 0)
            frames_on(1)
            p_forward(0)

        @pl.when(o == 4)
        def _():
            first_sums()

        @pl.when(o == 6)
        def _():
            c_step(1)
            p_landed(2, 0)
            p_start(2, 1)
            p_forward(1)
            p_forward(3)

        @pl.when(o == 7)
        def _():
            c_step(2)

        return factor_step(o, last, gm)

    @pl.when(core == 0)
    def _():
        frames_on(0)
        frames_on(1)
        ring_round(1)
        ring_round(2)
        first_sums()
        c_step(1)
        ring_round(3)
        c_step(2)
        second_sums()
        landed(gi, gi_recv)

    gi_copy = remote(gi, gi, gi_send, gi_recv, me, 0)

    @pl.when(core == 1)
    def _():
        p_landed(1, 0)
        p_start(1, 1)
        frames_on(0)
        landed(gm.at[pl.ds(0, RANK - 8), :], gf_recv)
        panels = RANK // PANEL
        gm[RANK - PANEL : RANK, :] = lax.fori_loop(0, panels, step, jnp.zeros((PANEL, RANK), jnp.float32))
        row_at = lax.broadcasted_iota(jnp.int32, (RANK, RANK), 0)
        lane_at = lax.broadcasted_iota(jnp.int32, (RANK, RANK), 1)
        factor = jnp.where(lane_at <= row_at, gm[...], 0.0)
        gi[...] = tn(factor, factor, HIGHEST)
        gi_copy.start()
        second_sums()

    c_landed(3, 0)
    c_landed(3, 1)
    c = cacc[6] + (cr[0, 3] + cr[1, 3])
    c = jnp.concatenate([c[:, 0:RANK], c[:, RANK:]], axis=0)
    w_ref[...] = nn(c, gi[...], HIGHEST)

    @pl.when(core == 0)
    def _():
        ring_landed(3)
        forward(ya.at[4, 0])

    @pl.when(core == 1)
    def _():
        p_landed(2, 1)
        p_forward(2)

    landed(ya.at[pl.ds(1, NZ - 1), sibling], fwd_recv)
    left(ya.at[pl.ds(1, NZ - 1), core], fwd_send)
    left(gz.at[pl.ds(0, NZ - 1)], gz_send)
    for s in range(4):
        c_copy(s, 0).wait_send()
        c_copy(s, 1).wait_send()
    left(yp.at[core], half_send)
    own_copy(0).wait()
    own_copy(1).wait()
    left(gr.at[pl.ds(0, PLANE - 1)], gf_send)
    left(gr.at[pl.ds(0, PLANE - 1)], g_send)
    left(yp.at[core, pl.ds(0, PLANE - 1)], y_send)
    left(vb, via_send)
    left(vb, on_send)
    left(xr.at[pl.ds(0, len(EARLY + LATE))], x_send)
    left(vb, x_send)

    @pl.when(core == 0)
    def _():
        gf_copy(my_d, 1).wait_send()
        for r in range(4):
            up_copy(r).wait_send()
            down_copy(r).wait_send()

    @pl.when(core == 1)
    def _():
        gi_copy.wait_send()
        left(ya.at[pl.ds(1, NZ - 1), 1, my_d], zd_send)
        for t in range(2):
            for q in range(2):
                left(p_size(1, t)[q], p1_send.at[t, q])
                left(p_size(2, t)[q], p2_send.at[t, q])


def rebuild_kernel(w_ref, y_ref, out_ref):
    my_z = (lax.axis_index("pos") // NX) % NZ
    wh, wl = halves(w_ref[...])
    both = jnp.concatenate([wh, wl], axis=0)
    for rel in range(NZ):
        yh, yl = halves(jnp.concatenate([y_ref[rel, q, x] for x in range(NX) for q in range(2)], axis=0))
        two = nt(both, yh)
        z = lax.rem(my_z + rel, NZ)
        lanes = pl.ds(pl.multiple_of(z * 64 * NX, 64 * NX), 64 * NX)
        out_ref[0, :, lanes] = two[0:64] + (two[64:128] + nt(wh, yl))


VMEM = pl.BlockSpec(memory_space=pltpu.VMEM)
ANY = pl.BlockSpec(memory_space=pl.ANY)
DMA = pltpu.SemaphoreType.DMA


def body(frames, sketch):
    x = frames.transpose(0, 2, 1).reshape(64 * 64, 128)
    s = sketch.reshape(NY, NZ, NX, 64, RANK)
    f32 = jnp.float32
    w, y_all = pl.pallas_call(
        main_kernel,
        out_shape=[
            jax.ShapeDtypeStruct((64, RANK), f32),
            jax.ShapeDtypeStruct((NZ, 2, PLANE, 32, RANK), f32),
        ],
        in_specs=[ANY, ANY],
        out_specs=[VMEM, ANY],
        scratch_shapes=[
            pltpu.VMEM((4096, 128), f32),
            pltpu.VMEM((4096, 128), f32),
            pltpu.VMEM((NY, NZ, NX, 64, RANK), jnp.bfloat16),
            pltpu.VMEM((PLANE, NZ, 32, 128), f32),
            pltpu.VMEM((PLANE, NZ, 32, 128), f32),
            pltpu.VMEM((64, RANK), f32),
            pltpu.VMEM((64, RANK), f32),
            pltpu.VMEM((64, RANK), f32),
            pltpu.VMEM((2, PLANE, 32, RANK), f32),
            pltpu.VMEM((RANK, RANK), f32),
            pltpu.VMEM((PLANE, 8, RANK), f32),
            pltpu.VMEM((8, RANK), f32),
            pltpu.VMEM((NZ, 8, RANK), f32),
            pltpu.VMEM((8, RANK), f32),
            pltpu.VMEM((RANK, RANK), f32),
            pltpu.VMEM((NZ, 32, 2 * RANK), f32),
            pltpu.VMEM((2, 4, 32, 2 * RANK), f32),
            pltpu.VMEM((len(TIES), 4, 32, 128), f32),
            pltpu.VMEM((RANK, RANK), f32),
            DMA, DMA, DMA, DMA,
            DMA, DMA((2,)), DMA, DMA, DMA, DMA, DMA((2,)),
            DMA, DMA, DMA, DMA, DMA, DMA, DMA((2, 4)), DMA((2, 4)),
            DMA((4,)), DMA((4,)), DMA((4,)), DMA((4,)),
            DMA, DMA, DMA((2, 2)), DMA((2, 2)), DMA((2, 2)), DMA((2, 2)), DMA, DMA,
            DMA, DMA((len(TIES),)), DMA, DMA, DMA,
        ],
        compiler_params=pltpu.CompilerParams(collective_id=0, has_side_effects=True, vmem_limit_bytes=58 << 20),
        cost_estimate=pl.CostEstimate(flops=4 * 10**9, bytes_accessed=3 * 10**7, transcendentals=0),
    )(x, s)
    y_all = y_all.reshape(NZ, 2, NY, NX, 32, RANK)
    return pl.pallas_call(
        rebuild_kernel,
        out_shape=jax.ShapeDtypeStruct((1, 64, 8192), f32),
        grid=(NY,),
        in_specs=[
            pl.BlockSpec((64, RANK), lambda i: (0, 0)),
            pl.BlockSpec((NZ, 2, None, NX, 32, RANK), lambda i: (0, 0, i, 0, 0, 0)),
        ],
        out_specs=pl.BlockSpec((1, 64, 2048), lambda i: (0, 0, i)),
        compiler_params=pltpu.CompilerParams(vmem_limit_bytes=58 << 20),
    )(w, y_all)


def solution(mesh):
    in_specs = (P("pos", None, "pix"), P(None, "pix", None))
    out_specs = P("pos", "pix", None)
    return jax.shard_map(body, mesh=mesh, in_specs=in_specs, out_specs=out_specs, check_vma=False)
```

```python
import jax
import jax.numpy as jnp
from jax import lax
from jax.experimental import pallas as pl
from jax.experimental.pallas import tpu as pltpu
from jax.sharding import PartitionSpec as P

MESH = pl.DeviceIdType.MESH
HIGHEST = lax.Precision.HIGHEST
NY, NZ, NX = 4, 8, 4
PLANE = NY * NX
RANK = 256
BLOCK, PANEL = 8, 32
TIES = [k for k in range(1, PLANE) if k // NX == 2 or k % NX == 2]
EARLY = [1, 3]
LATE = [k for k in range(1, PLANE) if k not in TIES + EARLY]


def tn(a, b, precision=None):
    return lax.dot_general(a, b, (((0,), (0,)), ((), ())), precision=precision, preferred_element_type=jnp.float32)


def nt(a, b, precision=None):
    return lax.dot_general(a, b, (((1,), (1,)), ((), ())), precision=precision, preferred_element_type=jnp.float32)


def nn(a, b, precision=None):
    return jnp.dot(a, b, precision=precision, preferred_element_type=jnp.float32)


def halves(a):
    high = a.astype(jnp.bfloat16)
    return high, (a - high.astype(jnp.float32)).astype(jnp.bfloat16)


def splat(rows, i):
    return jnp.broadcast_to(rows[:, i : i + 1], (BLOCK, 128))


def lanes_of(rows, base):
    tile = jnp.where(base < 128, rows[:, 0:128], rows[:, 128:256])
    return pltpu.roll(tile, lax.rem(256 - base, 128), 1)


def factor_diagonal(a):
    groups = [a[g * BLOCK : (g + 1) * BLOCK] for g in range(PANEL // BLOCK)]
    sub = lax.broadcasted_iota(jnp.int32, (BLOCK, 128), 0)
    for q in range(PANEL // BLOCK):
        rows = [jnp.broadcast_to(groups[q][k : k + 1, :], (BLOCK, 128)) for k in range(BLOCK)]
        columns = [[splat(groups[g], q * BLOCK + k) for k in range(BLOCK)] for g in range(q + 1, PANEL // BLOCK)]
        s = [[splat(rows[i], q * BLOCK + k) for k in range(i + 1)] for i in range(BLOCK)]
        inv, done = [], []
        for k in range(BLOCK):
            inv.append(lax.rsqrt(s[k][k]))
            for i in range(k + 1, BLOCK):
                s[i][k] = s[i][k] * inv[k]
            for i in range(k + 1, BLOCK):
                for m in range(k + 1, i + 1):
                    s[i][m] = s[i][m] - s[i][k] * s[m][k]
            row = rows[k]
            for i in range(k):
                row = row - s[k][i] * done[i]
            done.append(row * inv[k])
        for g in range(q + 1, PANEL // BLOCK):
            times = []
            for k in range(BLOCK):
                t = columns[g - q - 1][k]
                for i in range(k):
                    t = t - times[i] * s[k][i]
                times.append(t * inv[k])
                groups[g] = groups[g] - times[k] * done[k]
        block = done[0]
        for k in range(1, BLOCK):
            block = jnp.where(sub == k, done[k], block)
        groups[q] = block
    return jnp.concatenate(groups, axis=0)


def factor_step(o, last, a_ref):
    base = pl.multiple_of(o * PANEL, PANEL)
    lane = lax.broadcasted_iota(jnp.int32, (1, RANK), 1)
    before = (lane >= base - PANEL) & (lane < base)
    rows = jnp.where(before, 0.0, a_ref[pl.ds(base, PANEL), :])
    rows = rows - tn(lanes_of(last, base)[:, 0:PANEL], last, HIGHEST)
    row_at = lax.broadcasted_iota(jnp.int32, (PANEL, 128), 0)
    lane_at = lax.broadcasted_iota(jnp.int32, (PANEL, 128), 1)
    both = jnp.where(lane_at < PANEL, lanes_of(rows, base), jnp.where(lane_at == row_at + PANEL, 1.0, 0.0))
    both = factor_diagonal(both)
    inverse = jnp.where((lane_at >= PANEL) & (lane_at < 2 * PANEL), both, 0.0)
    own = (lane >= base) & (lane < base + PANEL)
    unit = lane == base + lax.broadcasted_iota(jnp.int32, (PANEL, 1), 0)
    rows = jnp.where(own, jnp.where(unit, 1.0, 0.0), rows)
    zeros = jnp.zeros((PANEL, RANK), jnp.float32)
    panel = nn(inverse, jnp.concatenate([zeros, rows, zeros, zeros], axis=0), HIGHEST)
    right = jnp.where(lane >= base, last, 0.0)
    below = lax.broadcasted_iota(jnp.int32, (RANK, 1), 0) >= base
    a_ref[...] = jnp.where(below & before, 0.0, a_ref[...]) - tn(right, last, HIGHEST)

    @pl.when(o > 0)
    def _():
        a_ref[pl.ds(pl.multiple_of(jnp.maximum(base - PANEL, 0), PANEL), PANEL), :] = last

    return panel


def main_kernel(
    x_hbm, s_hbm, w_ref, ya,
    xv, xt, sv, msg, xr, part, other, yl, yp, gl, gr, gp, gz, gf, gm, cacc, cr, vb, gi,
    x_in, s_in, pair_send, pair_recv, x_send, x_recv, y_send, y_recv, half_send, half_recv, own_sem,
    g_send, g_recv, gz_send, gz_recv, gf_send, gf_recv, c_send, c_recv,
    up_send, up_recv, down_send, down_recv, zd_send, zd_recv, p1_send, p1_recv, p2_send, p2_recv, fwd_send, fwd_recv,
    via_send, via_recv, on_send, gi_send, gi_recv,
):
    me = lax.axis_index("pos")
    core = lax.axis_index("pix")
    my_y, my_z, my_x = me // (NZ * NX), (me // NX) % NZ, me % NX
    my_d = my_y * NX + my_x
    sibling = 1 - core

    def at(y, z, x):
        return y * (NZ * NX) + z * NX + x

    def at_d(d):
        return at(d // NX, my_z, d % NX)

    def other_d(k):
        return lax.rem(my_y + k // NX, NY) * NX + lax.rem(my_x + k % NX, NX)

    def other_z(k):
        return lax.rem(my_z + k, NZ)

    def remote(src, dst, send_sem, recv_sem, pos, to_core):
        return pltpu.make_async_remote_copy(
            src_ref=src, dst_ref=dst, send_sem=send_sem, recv_sem=recv_sem,
            device_id={"pos": pos, "pix": to_core}, device_id_type=MESH,
        )

    def landed(ref, sem):
        remote(ref, ref, own_sem.at[0], sem, me, sibling).wait_recv()

    def left(ref, sem):
        remote(ref, ref, sem, own_sem.at[0], me, sibling).wait_send()

    x_copy_in = pltpu.make_async_copy(x_hbm, xv, x_in)
    x_copy_in.start()
    s_copy_in = pltpu.make_async_copy(s_hbm, sv, s_in)
    s_copy_in.start()

    barrier = pltpu.get_barrier_semaphore()

    def greet(pos, to_core):
        pl.semaphore_signal(barrier, inc=1, device_id={"pos": pos, "pix": to_core}, device_id_type=MESH)

    greet(me, sibling)

    @pl.loop(1, PLANE)
    def _(k):
        greet(at_d(other_d(k)), core)
        greet(at_d(other_d(k)), sibling)

    @pl.loop(1, NZ)
    def _(k):
        greet(at(my_y, other_z(k), my_x), core)

    x_copy_in.wait()

    @pl.loop(0, 32, unroll=4)
    def _(cp):
        low = xv[pl.ds(cp, 64, stride=64), :]
        high = xv[pl.ds(cp + 32, 64, stride=64), :]
        xt[pl.ds(pl.multiple_of(cp * 128, 128), 128), :] = jnp.concatenate([low, high], axis=0).T

    s_copy_in.wait()
    pl.semaphore_wait(barrier, 1 + 2 * (PLANE - 1) + NZ - 1)

    def x_copy(k, wave):
        d = other_d(k)
        if k in TIES:
            rows = pl.ds(0, 3) if wave == 0 else pl.ds(7, 1)
        else:
            rows = pl.ds(0, 5) if wave == 0 else pl.ds(5, 3)
        return remote(msg.at[d, rows], xr.at[my_d, rows], x_send, x_recv.at[wave], at_d(d), core)

    def via(k):
        return 3 if k // NX == 2 else k // NX, 3 if k % NX == 2 else k % NX

    def via_copy(n):
        k = TIES[n]
        vy, vx = via(k)
        pos = at(lax.rem(my_y + vy, NY), my_z, lax.rem(my_x + vx, NX))
        return remote(msg.at[other_d(k), pl.ds(3, 4)], vb.at[n], via_send, via_recv.at[n], pos, core)

    def on_copy(n, wave):
        k = TIES[n]
        vy, vx = via(k)
        from_d = lax.rem(my_y + NY - vy, NY) * NX + lax.rem(my_x + NX - vx, NX)
        pos = at(lax.rem(my_y + NY + k // NX - vy, NY), my_z, lax.rem(my_x + NX + k % NX - vx, NX))
        src, dst = vb.at[n, pl.ds(2 * wave, 2)], xr.at[from_d, pl.ds(3 + 2 * wave, 2)]
        return remote(src, dst, on_send, x_recv.at[wave], pos, core)

    total = jnp.zeros((64, RANK), jnp.float32)
    for k in TIES + EARLY + LATE + [0]:
        d = other_d(k)
        rows = [xt[pl.ds(at(d // NX, zz, d % NX), 32, stride=128), :] for zz in range(NZ)]
        for zz in range(NZ):
            msg[d, pl.ds(lax.rem(zz + 2 * NZ - 2 - my_z, NZ), 1)] = rows[zz].reshape(1, 32, 128)
        if k in TIES:
            via_copy(TIES.index(k)).start()
        if k in EARLY:
            x_copy(k, 0).start()
            x_copy(k, 1).start()
        xb = jnp.concatenate(rows, axis=0).T.astype(jnp.bfloat16)
        low = sv[d // NX, :, d % NX, 0:32, :].reshape(256, RANK)
        high = sv[d // NX, :, d % NX, 32:64, :].reshape(256, RANK)
        total = total + nn(xb[0:64], low) + nn(xb[64:128], high)
    part[...] = total
    pair = remote(part, other, pair_send, pair_recv, me, sibling)
    pair.start()
    xr[pl.ds(my_d, 1)] = msg[pl.ds(my_d, 1)]
    pair.wait()
    yl[...] = part[...] + other[...]
    my_half = pl.ds(pl.multiple_of(core * 32, 32), 32)
    yp[pl.ds(core, 1), pl.ds(my_d, 1)] = yl[my_half, :].reshape(1, 1, 32, RANK)
    gl[...] = tn(yl[...], yl[...], HIGHEST)

    def g_copy(k):
        d = other_d(k)
        rows = pl.ds(pl.multiple_of(core * 128 + d * 8, 8), 8)
        return remote(gl.at[rows, :], gr.at[my_d], g_send, g_recv, at_d(d), core)

    def gz_copy(k):
        z = other_z(k)
        return remote(gp, gz.at[my_z], gz_send, gz_recv, at(my_y, z, my_x), core)

    my_rows = pl.ds(pl.multiple_of((core * PLANE + my_d) * 8, 8), 8)

    def gf_copy(d, q):
        return remote(gf, gm.at[my_rows, :], gf_send, gf_recv, at_d(d), q)

    def y_copy(k):
        d = other_d(k)
        return remote(yl.at[my_half, :], yp.at[core, my_d], y_send, y_recv, at_d(d), core)

    half_copy = remote(yp.at[core], yp.at[core], half_send, half_recv, me, sibling)

    def own_copy(q):
        return pltpu.make_async_copy(yp.at[q], ya.at[0, q], own_sem.at[q])

    above, below = at(my_y, other_z(1), my_x), at(my_y, other_z(NZ - 1), my_x)

    def up_copy(r):
        src = yp.at[0] if r == 0 else ya.at[NZ - r, 0]
        dst = ya.at[NZ - 1 - r, 0]
        if r == 3:
            src, dst = src.at[pl.ds(0, 8)], dst.at[pl.ds(0, 8)]
        return remote(src, dst, up_send.at[r], up_recv.at[r], above, 0)

    def down_copy(r):
        src = yp.at[0] if r == 0 else ya.at[r, 0]
        dst = ya.at[1 + r, 0]
        if r == 3:
            src, dst = src.at[pl.ds(8, 8)], dst.at[pl.ds(8, 8)]
        return remote(src, dst, down_send.at[r], down_recv.at[r], below, 0)

    def forward(ref):
        remote(ref, ref, fwd_send, fwd_recv, me, sibling).start()

    def zd_copy(k):
        return remote(
            yl.at[my_half, :], ya.at[NZ - k, 1, my_d], zd_send, zd_recv, at(my_y, other_z(k), my_x), 1
        )

    near, far = pl.ds(1, 4), pl.ds(5, 3)

    upper, lower = pl.ds(0, 16), pl.ds(16, 16)

    def x_next(i):
        return lax.rem(my_x + i, NX)

    def y_next(i):
        return lax.rem(my_y + i, NY)

    def p1_copies(t):
        copies = []
        for q, (rel, block, along) in enumerate((
            (near, lambda i: my_y * NX + x_next(i), lambda i: at(my_y, my_z, x_next(i))),
            (far, lambda i: y_next(i) * NX + my_x, lambda i: at(y_next(i), my_z, my_x)),
        )):
            if t == 0:
                up, down = ya.at[rel, 1, block(0)], ya.at[rel, 1, block(0)]
            else:
                up, down = ya.at[rel, 1, block(3), upper], ya.at[rel, 1, block(1), lower]
            copies.append(remote(up, up, p1_send.at[t, q], p1_recv.at[t, q], along(1), 1))
            copies.append(remote(down, down, p1_send.at[t, q], p1_recv.at[t, q], along(3), 1))
        return copies

    def p2_copies(t):
        def row(i):
            return pl.ds(pl.multiple_of(y_next(i) * NX, NX), NX)

        copies = []
        if t == 0:
            up, down = ya.at[near, 1, row(0)], ya.at[near, 1, row(0)]
        else:
            up, down = ya.at[near, 1, row(3), upper], ya.at[near, 1, row(1), lower]
        copies.append(remote(up, up, p2_send.at[t, 0], p2_recv.at[t, 0], at(y_next(1), my_z, my_x), 1))
        copies.append(remote(down, down, p2_send.at[t, 0], p2_recv.at[t, 0], at(y_next(3), my_z, my_x), 1))
        for v in range(NY):
            if t == 0:
                up, down = ya.at[far, 1, v * NX + my_x], ya.at[far, 1, v * NX + my_x]
            else:
                up, down = ya.at[far, 1, v * NX + x_next(3), upper], ya.at[far, 1, v * NX + x_next(1), lower]
            copies.append(remote(up, up, p2_send.at[t, 1], p2_recv.at[t, 1], at(my_y, my_z, x_next(1)), 1))
            copies.append(remote(down, down, p2_send.at[t, 1], p2_recv.at[t, 1], at(my_y, my_z, x_next(3)), 1))
        return copies

    def p_forward(i):
        forward(ya.at[near, 1, pl.ds(pl.multiple_of(y_next(i) * NX, NX), NX)])
        for v in range(NY):
            forward(ya.at[far, 1, v * NX + x_next(i)])

    def p_size(phase, t):
        blocks = (1 if phase == 1 else 4) * (2 if t == 0 else 1)
        return [ya.at[near, 1, pl.ds(0, blocks)], ya.at[far, 1, pl.ds(0, blocks)]]

    def p_landed(phase, t):
        for q in range(2):
            landed(p_size(phase, t)[q], (p1_recv if phase == 1 else p2_recv).at[t, q])

    def p_start(phase, t):
        for copy in (p1_copies if phase == 1 else p2_copies)(t):
            copy.start()

    @pl.loop(1, PLANE)
    def _(k):
        g_copy(k).start()

    @pl.loop(1, PLANE)
    def _(k):
        y_copy(k).start()

    for k in LATE:
        x_copy(k, 0).start()
    gr[pl.ds(my_d, 1)] = gl[my_rows, :].reshape(1, 8, RANK)

    @pl.when(core == 1)
    def _():
        @pl.loop(1, NZ)
        def _(k):
            zd_copy(k).start()

    landed(gr.at[pl.ds(0, PLANE - 1)], g_recv)
    gp[...] = jnp.sum(gr[...], axis=0)

    @pl.loop(1, NZ)
    def _(k):
        gz_copy(k).start()

    gz[pl.ds(my_z, 1)] = gp[...].reshape(1, 8, RANK)
    landed(gz.at[pl.ds(0, NZ - 1)], gz_recv)
    gf[...] = jnp.sum(gz[...], axis=0)

    @pl.when(core == 0)
    def _():
        gf_copy(my_d, 1).start()

    @pl.loop(1, PLANE)
    def _(k):
        gf_copy(other_d(k), 1).start()

    gm[my_rows, :] = gf[...]
    landed(yp.at[core, pl.ds(0, PLANE - 1)], y_recv)
    half_copy.start()
    own_copy(core).start()

    @pl.when(core == 0)
    def _():
        up_copy(0).start()
        down_copy(0).start()

    @pl.when(core == 1)
    def _():
        landed(ya.at[pl.ds(1, NZ - 1), 1, my_d], zd_recv)
        p_start(1, 0)

    def frames_on(wave):
        if wave == 1:
            for k in LATE:
                x_copy(k, wave).start()
        for n in range(len(TIES)):
            if wave == 0:
                landed(vb.at[n], via_recv.at[n])
            on_copy(n, wave).start()
        for k in TIES:
            x_copy(k, wave).start()

    def ring_landed(r):
        if r < 3:
            landed(ya.at[NZ - 1 - r, 0], up_recv.at[r])
            landed(ya.at[1 + r, 0], down_recv.at[r])
        else:
            landed(ya.at[4, 0, pl.ds(0, 8)], up_recv.at[r])
            landed(ya.at[4, 0, pl.ds(8, 8)], down_recv.at[r])

    def ring_round(r):
        ring_landed(r - 1)
        up_copy(r).start()
        down_copy(r).start()
        forward(ya.at[NZ - r, 0])
        forward(ya.at[r, 0])

    def c_block(s, way):
        return pl.ds((2 - s if way == 0 else 2 + s) % NZ if s < 3 else (7 if way == 0 else 5), 1)

    def c_rows(s, way):
        return pl.ds(0, 32) if s else pl.ds(16 * way, 16)

    def c_copy(s, way):
        src, dst = cacc.at[c_block(s, way), c_rows(s, way)], cr.at[way, pl.ds(s, 1), c_rows(s, way)]
        return remote(src, dst, c_send.at[way, s], c_recv.at[way, s], above if way == 0 else below, core)

    def c_landed(s, way):
        landed(cr.at[way, pl.ds(s, 1), c_rows(s, way)], c_recv.at[way, s])

    def c_step(s):
        for way in range(2):
            if s:
                c_landed(s - 1, way)
                rows = c_rows(s - 1, way)
                cacc[c_block(s, way), rows] += cr[way, pl.ds(s - 1, 1), rows]
            c_copy(s, way).start()

    def coefficients(rows):
        ks = range(PLANE)
        total = jnp.zeros((rows.size * 32, 2 * RANK), jnp.float32)
        zero = jnp.zeros((64, RANK), jnp.float32)
        for n in range(0, len(ks), 2):
            lhs, rhs = [], []
            for k in ks[n : n + 2]:
                d = other_d(k)
                y = jnp.concatenate([yp[0, d], yp[1, d]], axis=0)
                lhs.append(xr[d, rows].reshape(rows.size * 32, 128))
                rhs.append(jnp.concatenate([y, zero], axis=1))
                rhs.append(jnp.concatenate([zero, y], axis=1))
            ah, al = halves(jnp.concatenate(lhs, axis=1))
            bh, bl = halves(jnp.concatenate(rhs, axis=0))
            total = total + (nn(ah, bh) + nn(ah, bl) + nn(al, bh))
        cacc[rows] = total.reshape(rows.size, 32, 2 * RANK)

    def first_sums():
        landed(yp.at[sibling], half_recv)
        own_copy(sibling).start()
        landed(xr.at[pl.ds(0, PLANE - 1), pl.ds(0, 5)], x_recv.at[0])
        coefficients(pl.ds(0, 5))
        c_step(0)

    def second_sums():
        landed(xr.at[pl.ds(0, PLANE - 1), pl.ds(0, 3)], x_recv.at[1])
        coefficients(pl.ds(5, 3))
        c_step(3)

    def step(o, last):
        @pl.when(o == 1)
        def _():
            p_landed(1, 1)
            p_start(2, 0)
            frames_on(1)
            p_forward(0)

        @pl.when(o == 4)
        def _():
            first_sums()

        @pl.when(o == 6)
        def _():
            c_step(1)
            p_landed(2, 0)
            p_start(2, 1)
            p_forward(1)
            p_forward(3)

        @pl.when(o == 7)
        def _():
            c_step(2)

        return factor_step(o, last, gm)

    @pl.when(core == 0)
    def _():
        frames_on(0)
        frames_on(1)
        ring_round(1)
        first_sums()
        ring_round(2)
        c_step(1)
        c_step(2)
        second_sums()
        ring_round(3)
        landed(gi, gi_recv)

    gi_copy = remote(gi, gi, gi_send, gi_recv, me, 0)

    @pl.when(core == 1)
    def _():
        p_landed(1, 0)
        p_start(1, 1)
        frames_on(0)
        landed(gm.at[pl.ds(0, RANK - 8), :], gf_recv)
        panels = RANK // PANEL
        gm[RANK - PANEL : RANK, :] = lax.fori_loop(0, panels, step, jnp.zeros((PANEL, RANK), jnp.float32))
        row_at = lax.broadcasted_iota(jnp.int32, (RANK, RANK), 0)
        lane_at = lax.broadcasted_iota(jnp.int32, (RANK, RANK), 1)
        factor = jnp.where(lane_at <= row_at, gm[...], 0.0)
        gi[...] = tn(factor, factor, HIGHEST)
        gi_copy.start()
        second_sums()

    c_landed(3, 0)
    c_landed(3, 1)
    c = cacc[6] + (cr[0, 3] + cr[1, 3])
    c = jnp.concatenate([c[:, 0:RANK], c[:, RANK:]], axis=0)
    w_ref[...] = nn(c, gi[...], HIGHEST)

    @pl.when(core == 0)
    def _():
        ring_landed(3)
        forward(ya.at[4, 0])

    @pl.when(core == 1)
    def _():
        p_landed(2, 1)
        p_forward(2)

    landed(ya.at[pl.ds(1, NZ - 1), sibling], fwd_recv)
    left(ya.at[pl.ds(1, NZ - 1), core], fwd_send)
    left(gz.at[pl.ds(0, NZ - 1)], gz_send)
    for s in range(4):
        c_copy(s, 0).wait_send()
        c_copy(s, 1).wait_send()
    left(yp.at[core], half_send)
    own_copy(0).wait()
    own_copy(1).wait()
    left(gr.at[pl.ds(0, PLANE - 1)], gf_send)
    left(gr.at[pl.ds(0, PLANE - 1)], g_send)
    left(yp.at[core, pl.ds(0, PLANE - 1)], y_send)
    left(vb, via_send)
    left(vb, on_send)
    left(xr.at[pl.ds(0, len(EARLY + LATE))], x_send)
    left(vb, x_send)

    @pl.when(core == 0)
    def _():
        gf_copy(my_d, 1).wait_send()
        for r in range(4):
            up_copy(r).wait_send()
            down_copy(r).wait_send()

    @pl.when(core == 1)
    def _():
        gi_copy.wait_send()
        left(ya.at[pl.ds(1, NZ - 1), 1, my_d], zd_send)
        for t in range(2):
            for q in range(2):
                left(p_size(1, t)[q], p1_send.at[t, q])
                left(p_size(2, t)[q], p2_send.at[t, q])


def rebuild_kernel(w_ref, y_ref, out_ref):
    my_z = (lax.axis_index("pos") // NX) % NZ
    wh, wl = halves(w_ref[...])
    both = jnp.concatenate([wh, wl], axis=0)
    for rel in range(NZ):
        yh, yl = halves(jnp.concatenate([y_ref[rel, q, x] for x in range(NX) for q in range(2)], axis=0))
        two = nt(both, yh)
        z = lax.rem(my_z + rel, NZ)
        lanes = pl.ds(pl.multiple_of(z * 64 * NX, 64 * NX), 64 * NX)
        out_ref[0, :, lanes] = two[0:64] + (two[64:128] + nt(wh, yl))


VMEM = pl.BlockSpec(memory_space=pltpu.VMEM)
ANY = pl.BlockSpec(memory_space=pl.ANY)
DMA = pltpu.SemaphoreType.DMA


def body(frames, sketch):
    x = frames.transpose(0, 2, 1).reshape(64 * 64, 128)
    s = sketch.reshape(NY, NZ, NX, 64, RANK)
    f32 = jnp.float32
    w, y_all = pl.pallas_call(
        main_kernel,
        out_shape=[
            jax.ShapeDtypeStruct((64, RANK), f32),
            jax.ShapeDtypeStruct((NZ, 2, PLANE, 32, RANK), f32),
        ],
        in_specs=[ANY, ANY],
        out_specs=[VMEM, ANY],
        scratch_shapes=[
            pltpu.VMEM((4096, 128), f32),
            pltpu.VMEM((4096, 128), f32),
            pltpu.VMEM((NY, NZ, NX, 64, RANK), jnp.bfloat16),
            pltpu.VMEM((PLANE, NZ, 32, 128), f32),
            pltpu.VMEM((PLANE, NZ, 32, 128), f32),
            pltpu.VMEM((64, RANK), f32),
            pltpu.VMEM((64, RANK), f32),
            pltpu.VMEM((64, RANK), f32),
            pltpu.VMEM((2, PLANE, 32, RANK), f32),
            pltpu.VMEM((RANK, RANK), f32),
            pltpu.VMEM((PLANE, 8, RANK), f32),
            pltpu.VMEM((8, RANK), f32),
            pltpu.VMEM((NZ, 8, RANK), f32),
            pltpu.VMEM((8, RANK), f32),
            pltpu.VMEM((RANK, RANK), f32),
            pltpu.VMEM((NZ, 32, 2 * RANK), f32),
            pltpu.VMEM((2, 4, 32, 2 * RANK), f32),
            pltpu.VMEM((len(TIES), 4, 32, 128), f32),
            pltpu.VMEM((RANK, RANK), f32),
            DMA, DMA, DMA, DMA,
            DMA, DMA((2,)), DMA, DMA, DMA, DMA, DMA((2,)),
            DMA, DMA, DMA, DMA, DMA, DMA, DMA((2, 4)), DMA((2, 4)),
            DMA((4,)), DMA((4,)), DMA((4,)), DMA((4,)),
            DMA, DMA, DMA((2, 2)), DMA((2, 2)), DMA((2, 2)), DMA((2, 2)), DMA, DMA,
            DMA, DMA((len(TIES),)), DMA, DMA, DMA,
        ],
        compiler_params=pltpu.CompilerParams(collective_id=0, has_side_effects=True, vmem_limit_bytes=58 << 20),
        cost_estimate=pl.CostEstimate(flops=4 * 10**9, bytes_accessed=3 * 10**7, transcendentals=0),
    )(x, s)
    y_all = y_all.reshape(NZ, 2, NY, NX, 32, RANK)
    return pl.pallas_call(
        rebuild_kernel,
        out_shape=jax.ShapeDtypeStruct((1, 64, 8192), f32),
        grid=(NY,),
        in_specs=[
            pl.BlockSpec((64, RANK), lambda i: (0, 0)),
            pl.BlockSpec((NZ, 2, None, NX, 32, RANK), lambda i: (0, 0, i, 0, 0, 0)),
        ],
        out_specs=pl.BlockSpec((1, 64, 2048), lambda i: (0, 0, i)),
        compiler_params=pltpu.CompilerParams(vmem_limit_bytes=58 << 20),
    )(w, y_all)


def solution(mesh):
    in_specs = (P("pos", None, "pix"), P(None, "pix", None))
    out_specs = P("pos", "pix", None)
    return jax.shard_map(body, mesh=mesh, in_specs=in_specs, out_specs=out_specs, check_vma=False)
```

```python
import jax
import jax.numpy as jnp
from jax import lax
from jax.experimental import pallas as pl
from jax.experimental.pallas import tpu as pltpu
from jax.sharding import PartitionSpec as P

MESH = pl.DeviceIdType.MESH
HIGHEST = lax.Precision.HIGHEST
NY, NZ, NX = 4, 8, 4
PLANE = NY * NX
RANK = 256
BLOCK, PANEL = 8, 32
TIES = [k for k in range(1, PLANE) if k // NX == 2 or k % NX == 2]
EARLY = [1, 3]
LATE = [k for k in range(1, PLANE) if k not in TIES + EARLY]


def tn(a, b, precision=None):
    return lax.dot_general(a, b, (((0,), (0,)), ((), ())), precision=precision, preferred_element_type=jnp.float32)


def nt(a, b, precision=None):
    return lax.dot_general(a, b, (((1,), (1,)), ((), ())), precision=precision, preferred_element_type=jnp.float32)


def nn(a, b, precision=None):
    return jnp.dot(a, b, precision=precision, preferred_element_type=jnp.float32)


def halves(a):
    high = a.astype(jnp.bfloat16)
    return high, (a - high.astype(jnp.float32)).astype(jnp.bfloat16)


def splat(rows, i):
    return jnp.broadcast_to(rows[:, i : i + 1], (BLOCK, 128))


def lanes_of(rows, base):
    tile = jnp.where(base < 128, rows[:, 0:128], rows[:, 128:256])
    return pltpu.roll(tile, lax.rem(256 - base, 128), 1)


def factor_diagonal(a):
    groups = [a[g * BLOCK : (g + 1) * BLOCK] for g in range(PANEL // BLOCK)]
    sub = lax.broadcasted_iota(jnp.int32, (BLOCK, 128), 0)
    for q in range(PANEL // BLOCK):
        rows = [jnp.broadcast_to(groups[q][k : k + 1, :], (BLOCK, 128)) for k in range(BLOCK)]
        columns = [[splat(groups[g], q * BLOCK + k) for k in range(BLOCK)] for g in range(q + 1, PANEL // BLOCK)]
        s = [[splat(rows[i], q * BLOCK + k) for k in range(i + 1)] for i in range(BLOCK)]
        inv, done = [], []
        for k in range(BLOCK):
            inv.append(lax.rsqrt(s[k][k]))
            for i in range(k + 1, BLOCK):
                s[i][k] = s[i][k] * inv[k]
            for i in range(k + 1, BLOCK):
                for m in range(k + 1, i + 1):
                    s[i][m] = s[i][m] - s[i][k] * s[m][k]
            row = rows[k]
            for i in range(k):
                row = row - s[k][i] * done[i]
            done.append(row * inv[k])
        for g in range(q + 1, PANEL // BLOCK):
            times = []
            for k in range(BLOCK):
                t = columns[g - q - 1][k]
                for i in range(k):
                    t = t - times[i] * s[k][i]
                times.append(t * inv[k])
                groups[g] = groups[g] - times[k] * done[k]
        block = done[0]
        for k in range(1, BLOCK):
            block = jnp.where(sub == k, done[k], block)
        groups[q] = block
    return jnp.concatenate(groups, axis=0)


def factor_step(o, last, a_ref):
    base = pl.multiple_of(o * PANEL, PANEL)
    lane = lax.broadcasted_iota(jnp.int32, (1, RANK), 1)
    before = (lane >= base - PANEL) & (lane < base)
    rows = jnp.where(before, 0.0, a_ref[pl.ds(base, PANEL), :])
    rows = rows - tn(lanes_of(last, base)[:, 0:PANEL], last, HIGHEST)
    row_at = lax.broadcasted_iota(jnp.int32, (PANEL, 128), 0)
    lane_at = lax.broadcasted_iota(jnp.int32, (PANEL, 128), 1)
    both = jnp.where(lane_at < PANEL, lanes_of(rows, base), jnp.where(lane_at == row_at + PANEL, 1.0, 0.0))
    both = factor_diagonal(both)
    inverse = jnp.where((lane_at >= PANEL) & (lane_at < 2 * PANEL), both, 0.0)
    own = (lane >= base) & (lane < base + PANEL)
    unit = lane == base + lax.broadcasted_iota(jnp.int32, (PANEL, 1), 0)
    rows = jnp.where(own, jnp.where(unit, 1.0, 0.0), rows)
    zeros = jnp.zeros((PANEL, RANK), jnp.float32)
    panel = nn(inverse, jnp.concatenate([zeros, rows, zeros, zeros], axis=0), HIGHEST)
    right = jnp.where(lane >= base, last, 0.0)
    below = lax.broadcasted_iota(jnp.int32, (RANK, 1), 0) >= base
    a_ref[...] = jnp.where(below & before, 0.0, a_ref[...]) - tn(right, last, HIGHEST)

    @pl.when(o > 0)
    def _():
        a_ref[pl.ds(pl.multiple_of(jnp.maximum(base - PANEL, 0), PANEL), PANEL), :] = last

    return panel


def main_kernel(
    x_hbm, s_hbm, w_ref, ya,
    xv, xt, sv, msg, xr, part, other, yl, yp, gl, gr, gp, gz, gf, gm, cacc, cr, vb, gi,
    x_in, s_in, pair_send, pair_recv, x_send, x_recv, y_send, y_recv, half_send, half_recv, own_sem,
    g_send, g_recv, gz_send, gz_recv, gf_send, gf_recv, c_send, c_recv,
    up_send, up_recv, down_send, down_recv, zd_send, zd_recv, p1_send, p1_recv, p2_send, p2_recv, fwd_send, fwd_recv,
    via_send, via_recv, on_send, gi_send, gi_recv,
):
    me = lax.axis_index("pos")
    core = lax.axis_index("pix")
    my_y, my_z, my_x = me // (NZ * NX), (me // NX) % NZ, me % NX
    my_d = my_y * NX + my_x
    sibling = 1 - core

    def at(y, z, x):
        return y * (NZ * NX) + z * NX + x

    def at_d(d):
        return at(d // NX, my_z, d % NX)

    def other_d(k):
        return lax.rem(my_y + k // NX, NY) * NX + lax.rem(my_x + k % NX, NX)

    def other_z(k):
        return lax.rem(my_z + k, NZ)

    def remote(src, dst, send_sem, recv_sem, pos, to_core):
        return pltpu.make_async_remote_copy(
            src_ref=src, dst_ref=dst, send_sem=send_sem, recv_sem=recv_sem,
            device_id={"pos": pos, "pix": to_core}, device_id_type=MESH,
        )

    def landed(ref, sem):
        remote(ref, ref, own_sem.at[0], sem, me, sibling).wait_recv()

    def left(ref, sem):
        remote(ref, ref, sem, own_sem.at[0], me, sibling).wait_send()

    x_copy_in = pltpu.make_async_copy(x_hbm, xv, x_in)
    x_copy_in.start()
    s_copy_in = pltpu.make_async_copy(s_hbm, sv, s_in)
    s_copy_in.start()

    barrier = pltpu.get_barrier_semaphore()

    def greet(pos, to_core):
        pl.semaphore_signal(barrier, inc=1, device_id={"pos": pos, "pix": to_core}, device_id_type=MESH)

    greet(me, sibling)

    @pl.loop(1, PLANE)
    def _(k):
        greet(at_d(other_d(k)), core)
        greet(at_d(other_d(k)), sibling)

    @pl.loop(1, NZ)
    def _(k):
        greet(at(my_y, other_z(k), my_x), core)

    x_copy_in.wait()

    @pl.loop(0, 32, unroll=4)
    def _(cp):
        low = xv[pl.ds(cp, 64, stride=64), :]
        high = xv[pl.ds(cp + 32, 64, stride=64), :]
        xt[pl.ds(pl.multiple_of(cp * 128, 128), 128), :] = jnp.concatenate([low, high], axis=0).T

    s_copy_in.wait()
    pl.semaphore_wait(barrier, 1 + 2 * (PLANE - 1) + NZ - 1)

    def x_copy(k, wave):
        d = other_d(k)
        if k in TIES:
            rows = pl.ds(0, 3) if wave == 0 else pl.ds(7, 1)
        else:
            rows = pl.ds(0, 5) if wave == 0 else pl.ds(5, 3)
        return remote(msg.at[d, rows], xr.at[my_d, rows], x_send, x_recv.at[wave], at_d(d), core)

    def via(k):
        return 3 if k // NX == 2 else k // NX, 3 if k % NX == 2 else k % NX

    def via_copy(n):
        k = TIES[n]
        vy, vx = via(k)
        pos = at(lax.rem(my_y + vy, NY), my_z, lax.rem(my_x + vx, NX))
        return remote(msg.at[other_d(k), pl.ds(3, 4)], vb.at[n], via_send, via_recv.at[n], pos, core)

    def on_copy(n, wave):
        k = TIES[n]
        vy, vx = via(k)
        from_d = lax.rem(my_y + NY - vy, NY) * NX + lax.rem(my_x + NX - vx, NX)
        pos = at(lax.rem(my_y + NY + k // NX - vy, NY), my_z, lax.rem(my_x + NX + k % NX - vx, NX))
        src, dst = vb.at[n, pl.ds(2 * wave, 2)], xr.at[from_d, pl.ds(3 + 2 * wave, 2)]
        return remote(src, dst, on_send, x_recv.at[wave], pos, core)

    total = jnp.zeros((64, RANK), jnp.float32)
    for k in TIES + EARLY + LATE + [0]:
        d = other_d(k)
        rows = [xt[pl.ds(at(d // NX, zz, d % NX), 32, stride=128), :] for zz in range(NZ)]
        for zz in range(NZ):
            msg[d, pl.ds(lax.rem(zz + 2 * NZ - 2 - my_z, NZ), 1)] = rows[zz].reshape(1, 32, 128)
        if k in TIES:
            via_copy(TIES.index(k)).start()
        if k in EARLY:
            x_copy(k, 0).start()
            x_copy(k, 1).start()
        xb = jnp.concatenate(rows, axis=0).T.astype(jnp.bfloat16)
        low = sv[d // NX, :, d % NX, 0:32, :].reshape(256, RANK)
        high = sv[d // NX, :, d % NX, 32:64, :].reshape(256, RANK)
        total = total + nn(xb[0:64], low) + nn(xb[64:128], high)
    part[...] = total
    pair = remote(part, other, pair_send, pair_recv, me, sibling)
    pair.start()
    xr[pl.ds(my_d, 1)] = msg[pl.ds(my_d, 1)]
    pair.wait()
    yl[...] = part[...] + other[...]
    my_half = pl.ds(pl.multiple_of(core * 32, 32), 32)
    yp[pl.ds(core, 1), pl.ds(my_d, 1)] = yl[my_half, :].reshape(1, 1, 32, RANK)
    gl[...] = tn(yl[...], yl[...], HIGHEST)

    def g_copy(k):
        d = other_d(k)
        rows = pl.ds(pl.multiple_of(core * 128 + d * 8, 8), 8)
        return remote(gl.at[rows, :], gr.at[my_d], g_send, g_recv, at_d(d), core)

    def gz_copy(k):
        z = other_z(k)
        return remote(gp, gz.at[my_z], gz_send, gz_recv, at(my_y, z, my_x), core)

    my_rows = pl.ds(pl.multiple_of((core * PLANE + my_d) * 8, 8), 8)

    def gf_copy(d, q):
        return remote(gf, gm.at[my_rows, :], gf_send, gf_recv, at_d(d), q)

    def y_copy(k):
        d = other_d(k)
        return remote(yl.at[my_half, :], yp.at[core, my_d], y_send, y_recv, at_d(d), core)

    half_copy = remote(yp.at[core], yp.at[core], half_send, half_recv, me, sibling)

    def own_copy(q):
        return pltpu.make_async_copy(yp.at[q], ya.at[0, q], own_sem.at[q])

    above, below = at(my_y, other_z(1), my_x), at(my_y, other_z(NZ - 1), my_x)

    def up_copy(r):
        src = yp.at[0] if r == 0 else ya.at[NZ - r, 0]
        dst = ya.at[NZ - 1 - r, 0]
        if r == 3:
            src, dst = src.at[pl.ds(0, 8)], dst.at[pl.ds(0, 8)]
        return remote(src, dst, up_send.at[r], up_recv.at[r], above, 0)

    def down_copy(r):
        src = yp.at[0] if r == 0 else ya.at[r, 0]
        dst = ya.at[1 + r, 0]
        if r == 3:
            src, dst = src.at[pl.ds(8, 8)], dst.at[pl.ds(8, 8)]
        return remote(src, dst, down_send.at[r], down_recv.at[r], below, 0)

    def forward(ref):
        remote(ref, ref, fwd_send, fwd_recv, me, sibling).start()

    def zd_copy(k):
        return remote(
            yl.at[my_half, :], ya.at[NZ - k, 1, my_d], zd_send, zd_recv, at(my_y, other_z(k), my_x), 1
        )

    near, far = pl.ds(1, 4), pl.ds(5, 3)

    upper, lower = pl.ds(0, 16), pl.ds(16, 16)

    def x_next(i):
        return lax.rem(my_x + i, NX)

    def y_next(i):
        return lax.rem(my_y + i, NY)

    def p1_copies(t):
        copies = []
        for q, (rel, block, along) in enumerate((
            (near, lambda i: my_y * NX + x_next(i), lambda i: at(my_y, my_z, x_next(i))),
            (far, lambda i: y_next(i) * NX + my_x, lambda i: at(y_next(i), my_z, my_x)),
        )):
            if t == 0:
                up, down = ya.at[rel, 1, block(0)], ya.at[rel, 1, block(0)]
            else:
                up, down = ya.at[rel, 1, block(3), upper], ya.at[rel, 1, block(1), lower]
            copies.append(remote(up, up, p1_send.at[t, q], p1_recv.at[t, q], along(1), 1))
            copies.append(remote(down, down, p1_send.at[t, q], p1_recv.at[t, q], along(3), 1))
        return copies

    def p2_copies(t):
        def row(i):
            return pl.ds(pl.multiple_of(y_next(i) * NX, NX), NX)

        copies = []
        if t == 0:
            up, down = ya.at[near, 1, row(0)], ya.at[near, 1, row(0)]
        else:
            up, down = ya.at[near, 1, row(3), upper], ya.at[near, 1, row(1), lower]
        copies.append(remote(up, up, p2_send.at[t, 0], p2_recv.at[t, 0], at(y_next(1), my_z, my_x), 1))
        copies.append(remote(down, down, p2_send.at[t, 0], p2_recv.at[t, 0], at(y_next(3), my_z, my_x), 1))
        for v in range(NY):
            if t == 0:
                up, down = ya.at[far, 1, v * NX + my_x], ya.at[far, 1, v * NX + my_x]
            else:
                up, down = ya.at[far, 1, v * NX + x_next(3), upper], ya.at[far, 1, v * NX + x_next(1), lower]
            copies.append(remote(up, up, p2_send.at[t, 1], p2_recv.at[t, 1], at(my_y, my_z, x_next(1)), 1))
            copies.append(remote(down, down, p2_send.at[t, 1], p2_recv.at[t, 1], at(my_y, my_z, x_next(3)), 1))
        return copies

    def p_forward(i):
        forward(ya.at[near, 1, pl.ds(pl.multiple_of(y_next(i) * NX, NX), NX)])
        for v in range(NY):
            forward(ya.at[far, 1, v * NX + x_next(i)])

    def p_size(phase, t):
        blocks = (1 if phase == 1 else 4) * (2 if t == 0 else 1)
        return [ya.at[near, 1, pl.ds(0, blocks)], ya.at[far, 1, pl.ds(0, blocks)]]

    def p_landed(phase, t):
        for q in range(2):
            landed(p_size(phase, t)[q], (p1_recv if phase == 1 else p2_recv).at[t, q])

    def p_start(phase, t):
        for copy in (p1_copies if phase == 1 else p2_copies)(t):
            copy.start()

    @pl.loop(1, PLANE)
    def _(k):
        g_copy(k).start()

    @pl.loop(1, PLANE)
    def _(k):
        y_copy(k).start()

    for k in LATE:
        x_copy(k, 0).start()
    gr[pl.ds(my_d, 1)] = gl[my_rows, :].reshape(1, 8, RANK)

    @pl.when(core == 1)
    def _():
        @pl.loop(1, NZ)
        def _(k):
            zd_copy(k).start()

    landed(gr.at[pl.ds(0, PLANE - 1)], g_recv)
    gp[...] = jnp.sum(gr[...], axis=0)

    @pl.loop(1, NZ)
    def _(k):
        gz_copy(k).start()

    gz[pl.ds(my_z, 1)] = gp[...].reshape(1, 8, RANK)
    landed(gz.at[pl.ds(0, NZ - 1)], gz_recv)
    gf[...] = jnp.sum(gz[...], axis=0)

    @pl.when(core == 0)
    def _():
        gf_copy(my_d, 1).start()

    @pl.loop(1, PLANE)
    def _(k):
        gf_copy(other_d(k), 1).start()

    gm[my_rows, :] = gf[...]
    landed(yp.at[core, pl.ds(0, PLANE - 1)], y_recv)
    half_copy.start()
    own_copy(core).start()

    @pl.when(core == 0)
    def _():
        up_copy(0).start()
        down_copy(0).start()

    @pl.when(core == 1)
    def _():
        landed(ya.at[pl.ds(1, NZ - 1), 1, my_d], zd_recv)
        p_start(1, 0)

    def frames_on(wave):
        if wave == 1:
            for k in LATE:
                x_copy(k, wave).start()
        for n in range(len(TIES)):
            if wave == 0:
                landed(vb.at[n], via_recv.at[n])
            on_copy(n, wave).start()
        for k in TIES:
            x_copy(k, wave).start()

    def ring_landed(r):
        if r < 3:
            landed(ya.at[NZ - 1 - r, 0], up_recv.at[r])
            landed(ya.at[1 + r, 0], down_recv.at[r])
        else:
            landed(ya.at[4, 0, pl.ds(0, 8)], up_recv.at[r])
            landed(ya.at[4, 0, pl.ds(8, 8)], down_recv.at[r])

    def ring_round(r):
        ring_landed(r - 1)
        up_copy(r).start()
        down_copy(r).start()

    def ring_forward(r):
        forward(ya.at[NZ - r, 0])
        forward(ya.at[r, 0])

    def c_block(s, way):
        return pl.ds((2 - s if way == 0 else 2 + s) % NZ if s < 3 else (7 if way == 0 else 5), 1)

    def c_rows(s, way):
        return pl.ds(0, 32) if s else pl.ds(16 * way, 16)

    def c_copy(s, way):
        src, dst = cacc.at[c_block(s, way), c_rows(s, way)], cr.at[way, pl.ds(s, 1), c_rows(s, way)]
        return remote(src, dst, c_send.at[way, s], c_recv.at[way, s], above if way == 0 else below, core)

    def c_landed(s, way):
        landed(cr.at[way, pl.ds(s, 1), c_rows(s, way)], c_recv.at[way, s])

    def c_step(s):
        for way in range(2):
            if s:
                c_landed(s - 1, way)
                rows = c_rows(s - 1, way)
                cacc[c_block(s, way), rows] += cr[way, pl.ds(s - 1, 1), rows]
            c_copy(s, way).start()

    def coefficients(rows):
        ks = range(PLANE)
        total = jnp.zeros((rows.size * 32, 2 * RANK), jnp.float32)
        zero = jnp.zeros((64, RANK), jnp.float32)
        for n in range(0, len(ks), 2):
            lhs, rhs = [], []
            for k in ks[n : n + 2]:
                d = other_d(k)
                y = jnp.concatenate([yp[0, d], yp[1, d]], axis=0)
                lhs.append(xr[d, rows].reshape(rows.size * 32, 128))
                rhs.append(jnp.concatenate([y, zero], axis=1))
                rhs.append(jnp.concatenate([zero, y], axis=1))
            ah, al = halves(jnp.concatenate(lhs, axis=1))
            bh, bl = halves(jnp.concatenate(rhs, axis=0))
            total = total + (nn(ah, bh) + nn(ah, bl) + nn(al, bh))
        cacc[rows] = total.reshape(rows.size, 32, 2 * RANK)

    def first_sums():
        landed(yp.at[sibling], half_recv)
        own_copy(sibling).start()
        landed(xr.at[pl.ds(0, PLANE - 1), pl.ds(0, 5)], x_recv.at[0])
        coefficients(pl.ds(0, 5))
        c_step(0)

    def second_sums():
        landed(xr.at[pl.ds(0, PLANE - 1), pl.ds(0, 3)], x_recv.at[1])
        coefficients(pl.ds(5, 3))
        c_step(3)

    def step(o, last):
        @pl.when(o == 1)
        def _():
            p_landed(1, 1)
            p_start(2, 0)
            frames_on(1)
            p_forward(0)

        @pl.when(o == 4)
        def _():
            first_sums()

        @pl.when(o == 6)
        def _():
            c_step(1)
            p_landed(2, 0)
            p_start(2, 1)
            p_forward(1)
            p_forward(3)

        @pl.when(o == 7)
        def _():
            c_step(2)

        return factor_step(o, last, gm)

    @pl.when(core == 0)
    def _():
        frames_on(0)
        ring_round(1)
        frames_on(1)
        ring_forward(1)
        first_sums()
        ring_round(2)
        c_step(1)
        ring_forward(2)
        c_step(2)
        second_sums()
        ring_round(3)
        ring_forward(3)
        landed(gi, gi_recv)

    gi_copy = remote(gi, gi, gi_send, gi_recv, me, 0)

    @pl.when(core == 1)
    def _():
        p_landed(1, 0)
        p_start(1, 1)
        frames_on(0)
        landed(gm.at[pl.ds(0, RANK - 8), :], gf_recv)
        panels = RANK // PANEL
        gm[RANK - PANEL : RANK, :] = lax.fori_loop(0, panels, step, jnp.zeros((PANEL, RANK), jnp.float32))
        row_at = lax.broadcasted_iota(jnp.int32, (RANK, RANK), 0)
        lane_at = lax.broadcasted_iota(jnp.int32, (RANK, RANK), 1)
        factor = jnp.where(lane_at <= row_at, gm[...], 0.0)
        gi[...] = tn(factor, factor, HIGHEST)
        gi_copy.start()
        second_sums()

    c_landed(3, 0)
    c_landed(3, 1)
    c = cacc[6] + (cr[0, 3] + cr[1, 3])
    c = jnp.concatenate([c[:, 0:RANK], c[:, RANK:]], axis=0)
    w_ref[...] = nn(c, gi[...], HIGHEST)

    @pl.when(core == 0)
    def _():
        ring_landed(3)
        forward(ya.at[4, 0])

    @pl.when(core == 1)
    def _():
        p_landed(2, 1)
        p_forward(2)

    landed(ya.at[pl.ds(1, NZ - 1), sibling], fwd_recv)
    left(ya.at[pl.ds(1, NZ - 1), core], fwd_send)
    left(gz.at[pl.ds(0, NZ - 1)], gz_send)
    for s in range(4):
        c_copy(s, 0).wait_send()
        c_copy(s, 1).wait_send()
    left(yp.at[core], half_send)
    own_copy(0).wait()
    own_copy(1).wait()
    left(gr.at[pl.ds(0, PLANE - 1)], gf_send)
    left(gr.at[pl.ds(0, PLANE - 1)], g_send)
    left(yp.at[core, pl.ds(0, PLANE - 1)], y_send)
    left(vb, via_send)
    left(vb, on_send)
    left(xr.at[pl.ds(0, len(EARLY + LATE))], x_send)
    left(vb, x_send)

    @pl.when(core == 0)
    def _():
        gf_copy(my_d, 1).wait_send()
        for r in range(4):
            up_copy(r).wait_send()
            down_copy(r).wait_send()

    @pl.when(core == 1)
    def _():
        gi_copy.wait_send()
        left(ya.at[pl.ds(1, NZ - 1), 1, my_d], zd_send)
        for t in range(2):
            for q in range(2):
                left(p_size(1, t)[q], p1_send.at[t, q])
                left(p_size(2, t)[q], p2_send.at[t, q])


def rebuild_kernel(w_ref, y_ref, out_ref):
    my_z = (lax.axis_index("pos") // NX) % NZ
    wh, wl = halves(w_ref[...])
    both = jnp.concatenate([wh, wl], axis=0)
    for rel in range(NZ):
        yh, yl = halves(jnp.concatenate([y_ref[rel, q, x] for x in range(NX) for q in range(2)], axis=0))
        two = nt(both, yh)
        z = lax.rem(my_z + rel, NZ)
        lanes = pl.ds(pl.multiple_of(z * 64 * NX, 64 * NX), 64 * NX)
        out_ref[0, :, lanes] = two[0:64] + (two[64:128] + nt(wh, yl))


VMEM = pl.BlockSpec(memory_space=pltpu.VMEM)
ANY = pl.BlockSpec(memory_space=pl.ANY)
DMA = pltpu.SemaphoreType.DMA


def body(frames, sketch):
    x = frames.transpose(0, 2, 1).reshape(64 * 64, 128)
    s = sketch.reshape(NY, NZ, NX, 64, RANK)
    f32 = jnp.float32
    w, y_all = pl.pallas_call(
        main_kernel,
        out_shape=[
            jax.ShapeDtypeStruct((64, RANK), f32),
            jax.ShapeDtypeStruct((NZ, 2, PLANE, 32, RANK), f32),
        ],
        in_specs=[ANY, ANY],
        out_specs=[VMEM, ANY],
        scratch_shapes=[
            pltpu.VMEM((4096, 128), f32),
            pltpu.VMEM((4096, 128), f32),
            pltpu.VMEM((NY, NZ, NX, 64, RANK), jnp.bfloat16),
            pltpu.VMEM((PLANE, NZ, 32, 128), f32),
            pltpu.VMEM((PLANE, NZ, 32, 128), f32),
            pltpu.VMEM((64, RANK), f32),
            pltpu.VMEM((64, RANK), f32),
            pltpu.VMEM((64, RANK), f32),
            pltpu.VMEM((2, PLANE, 32, RANK), f32),
            pltpu.VMEM((RANK, RANK), f32),
            pltpu.VMEM((PLANE, 8, RANK), f32),
            pltpu.VMEM((8, RANK), f32),
            pltpu.VMEM((NZ, 8, RANK), f32),
            pltpu.VMEM((8, RANK), f32),
            pltpu.VMEM((RANK, RANK), f32),
            pltpu.VMEM((NZ, 32, 2 * RANK), f32),
            pltpu.VMEM((2, 4, 32, 2 * RANK), f32),
            pltpu.VMEM((len(TIES), 4, 32, 128), f32),
            pltpu.VMEM((RANK, RANK), f32),
            DMA, DMA, DMA, DMA,
            DMA, DMA((2,)), DMA, DMA, DMA, DMA, DMA((2,)),
            DMA, DMA, DMA, DMA, DMA, DMA, DMA((2, 4)), DMA((2, 4)),
            DMA((4,)), DMA((4,)), DMA((4,)), DMA((4,)),
            DMA, DMA, DMA((2, 2)), DMA((2, 2)), DMA((2, 2)), DMA((2, 2)), DMA, DMA,
            DMA, DMA((len(TIES),)), DMA, DMA, DMA,
        ],
        compiler_params=pltpu.CompilerParams(collective_id=0, has_side_effects=True, vmem_limit_bytes=58 << 20),
        cost_estimate=pl.CostEstimate(flops=4 * 10**9, bytes_accessed=3 * 10**7, transcendentals=0),
    )(x, s)
    y_all = y_all.reshape(NZ, 2, NY, NX, 32, RANK)
    return pl.pallas_call(
        rebuild_kernel,
        out_shape=jax.ShapeDtypeStruct((1, 64, 8192), f32),
        grid=(NY,),
        in_specs=[
            pl.BlockSpec((64, RANK), lambda i: (0, 0)),
            pl.BlockSpec((NZ, 2, None, NX, 32, RANK), lambda i: (0, 0, i, 0, 0, 0)),
        ],
        out_specs=pl.BlockSpec((1, 64, 2048), lambda i: (0, 0, i)),
        compiler_params=pltpu.CompilerParams(vmem_limit_bytes=58 << 20),
    )(w, y_all)


def solution(mesh):
    in_specs = (P("pos", None, "pix"), P(None, "pix", None))
    out_specs = P("pos", "pix", None)
    return jax.shard_map(body, mesh=mesh, in_specs=in_specs, out_specs=out_specs, check_vma=False)
```

```python
import jax
import jax.numpy as jnp
from jax import lax
from jax.experimental import pallas as pl
from jax.experimental.pallas import tpu as pltpu
from jax.sharding import PartitionSpec as P

MESH = pl.DeviceIdType.MESH
HIGHEST = lax.Precision.HIGHEST
NY, NZ, NX = 4, 8, 4
PLANE = NY * NX
RANK = 256
BLOCK, PANEL = 8, 32
TIES = [k for k in range(1, PLANE) if k // NX == 2 or k % NX == 2]
EARLY = [1, 3]
LATE = [k for k in range(1, PLANE) if k not in TIES + EARLY]


def tn(a, b, precision=None):
    return lax.dot_general(a, b, (((0,), (0,)), ((), ())), precision=precision, preferred_element_type=jnp.float32)


def nt(a, b, precision=None):
    return lax.dot_general(a, b, (((1,), (1,)), ((), ())), precision=precision, preferred_element_type=jnp.float32)


def nn(a, b, precision=None):
    return jnp.dot(a, b, precision=precision, preferred_element_type=jnp.float32)


def halves(a):
    high = a.astype(jnp.bfloat16)
    return high, (a - high.astype(jnp.float32)).astype(jnp.bfloat16)


def splat(rows, i):
    return jnp.broadcast_to(rows[:, i : i + 1], (BLOCK, 128))


def lanes_of(rows, base):
    tile = jnp.where(base < 128, rows[:, 0:128], rows[:, 128:256])
    return pltpu.roll(tile, lax.rem(256 - base, 128), 1)


def factor_diagonal(a):
    groups = [a[g * BLOCK : (g + 1) * BLOCK] for g in range(PANEL // BLOCK)]
    sub = lax.broadcasted_iota(jnp.int32, (BLOCK, 128), 0)
    for q in range(PANEL // BLOCK):
        rows = [jnp.broadcast_to(groups[q][k : k + 1, :], (BLOCK, 128)) for k in range(BLOCK)]
        columns = [[splat(groups[g], q * BLOCK + k) for k in range(BLOCK)] for g in range(q + 1, PANEL // BLOCK)]
        s = [[splat(rows[i], q * BLOCK + k) for k in range(i + 1)] for i in range(BLOCK)]
        inv, done = [], []
        for k in range(BLOCK):
            inv.append(lax.rsqrt(s[k][k]))
            for i in range(k + 1, BLOCK):
                s[i][k] = s[i][k] * inv[k]
            for i in range(k + 1, BLOCK):
                for m in range(k + 1, i + 1):
                    s[i][m] = s[i][m] - s[i][k] * s[m][k]
            row = rows[k]
            for i in range(k):
                row = row - s[k][i] * done[i]
            done.append(row * inv[k])
        for g in range(q + 1, PANEL // BLOCK):
            times = []
            for k in range(BLOCK):
                t = columns[g - q - 1][k]
                for i in range(k):
                    t = t - times[i] * s[k][i]
                times.append(t * inv[k])
                groups[g] = groups[g] - times[k] * done[k]
        block = done[0]
        for k in range(1, BLOCK):
            block = jnp.where(sub == k, done[k], block)
        groups[q] = block
    return jnp.concatenate(groups, axis=0)


def factor_step(o, last, a_ref):
    base = pl.multiple_of(o * PANEL, PANEL)
    lane = lax.broadcasted_iota(jnp.int32, (1, RANK), 1)
    before = (lane >= base - PANEL) & (lane < base)
    rows = jnp.where(before, 0.0, a_ref[pl.ds(base, PANEL), :])
    rows = rows - tn(lanes_of(last, base)[:, 0:PANEL], last, HIGHEST)
    row_at = lax.broadcasted_iota(jnp.int32, (PANEL, 128), 0)
    lane_at = lax.broadcasted_iota(jnp.int32, (PANEL, 128), 1)
    both = jnp.where(lane_at < PANEL, lanes_of(rows, base), jnp.where(lane_at == row_at + PANEL, 1.0, 0.0))
    both = factor_diagonal(both)
    inverse = jnp.where((lane_at >= PANEL) & (lane_at < 2 * PANEL), both, 0.0)
    own = (lane >= base) & (lane < base + PANEL)
    unit = lane == base + lax.broadcasted_iota(jnp.int32, (PANEL, 1), 0)
    rows = jnp.where(own, jnp.where(unit, 1.0, 0.0), rows)
    zeros = jnp.zeros((PANEL, RANK), jnp.float32)
    panel = nn(inverse, jnp.concatenate([zeros, rows, zeros, zeros], axis=0), HIGHEST)
    right = jnp.where(lane >= base, last, 0.0)
    below = lax.broadcasted_iota(jnp.int32, (RANK, 1), 0) >= base
    a_ref[...] = jnp.where(below & before, 0.0, a_ref[...]) - tn(right, last, HIGHEST)

    @pl.when(o > 0)
    def _():
        a_ref[pl.ds(pl.multiple_of(jnp.maximum(base - PANEL, 0), PANEL), PANEL), :] = last

    return panel


def main_kernel(
    x_hbm, s_hbm, w_ref, ya,
    xv, xt, sv, msg, xr, part, other, yl, yp, gl, gr, gp, gz, gf, gm, cacc, cr, vb, gi,
    x_in, s_in, pair_send, pair_recv, x_send, x_recv, y_send, y_recv, half_send, half_recv, own_sem,
    g_send, g_recv, gz_send, gz_recv, gf_send, gf_recv, c_send, c_recv,
    up_send, up_recv, down_send, down_recv, zd_send, zd_recv, p1_send, p1_recv, p2_send, p2_recv, fwd_send, fwd_recv,
    via_send, via_recv, on_send, gi_send, gi_recv,
):
    me = lax.axis_index("pos")
    core = lax.axis_index("pix")
    my_y, my_z, my_x = me // (NZ * NX), (me // NX) % NZ, me % NX
    my_d = my_y * NX + my_x
    sibling = 1 - core

    def at(y, z, x):
        return y * (NZ * NX) + z * NX + x

    def at_d(d):
        return at(d // NX, my_z, d % NX)

    def other_d(k):
        return lax.rem(my_y + k // NX, NY) * NX + lax.rem(my_x + k % NX, NX)

    def other_z(k):
        return lax.rem(my_z + k, NZ)

    def remote(src, dst, send_sem, recv_sem, pos, to_core):
        return pltpu.make_async_remote_copy(
            src_ref=src, dst_ref=dst, send_sem=send_sem, recv_sem=recv_sem,
            device_id={"pos": pos, "pix": to_core}, device_id_type=MESH,
        )

    def landed(ref, sem):
        remote(ref, ref, own_sem.at[0], sem, me, sibling).wait_recv()

    def left(ref, sem):
        remote(ref, ref, sem, own_sem.at[0], me, sibling).wait_send()

    x_copy_in = pltpu.make_async_copy(x_hbm, xv, x_in)
    x_copy_in.start()
    s_copy_in = pltpu.make_async_copy(s_hbm, sv, s_in)
    s_copy_in.start()

    barrier = pltpu.get_barrier_semaphore()

    def greet(pos, to_core):
        pl.semaphore_signal(barrier, inc=1, device_id={"pos": pos, "pix": to_core}, device_id_type=MESH)

    greet(me, sibling)

    @pl.loop(1, PLANE)
    def _(k):
        greet(at_d(other_d(k)), core)
        greet(at_d(other_d(k)), sibling)

    @pl.loop(1, NZ)
    def _(k):
        greet(at(my_y, other_z(k), my_x), core)

    x_copy_in.wait()

    @pl.loop(0, 32, unroll=4)
    def _(cp):
        low = xv[pl.ds(cp, 64, stride=64), :]
        high = xv[pl.ds(cp + 32, 64, stride=64), :]
        xt[pl.ds(pl.multiple_of(cp * 128, 128), 128), :] = jnp.concatenate([low, high], axis=0).T

    s_copy_in.wait()
    pl.semaphore_wait(barrier, 1 + 2 * (PLANE - 1) + NZ - 1)

    def x_copy(k, wave):
        d = other_d(k)
        if k in TIES:
            rows = pl.ds(0, 3) if wave == 0 else pl.ds(7, 1)
        else:
            rows = pl.ds(0, 5) if wave == 0 else pl.ds(5, 3)
        return remote(msg.at[d, rows], xr.at[my_d, rows], x_send, x_recv.at[wave], at_d(d), core)

    def via(k):
        return 3 if k // NX == 2 else k // NX, 3 if k % NX == 2 else k % NX

    def via_copy(n):
        k = TIES[n]
        vy, vx = via(k)
        pos = at(lax.rem(my_y + vy, NY), my_z, lax.rem(my_x + vx, NX))
        return remote(msg.at[other_d(k), pl.ds(3, 4)], vb.at[n], via_send, via_recv.at[n], pos, core)

    def on_copy(n, wave):
        k = TIES[n]
        vy, vx = via(k)
        from_d = lax.rem(my_y + NY - vy, NY) * NX + lax.rem(my_x + NX - vx, NX)
        pos = at(lax.rem(my_y + NY + k // NX - vy, NY), my_z, lax.rem(my_x + NX + k % NX - vx, NX))
        src, dst = vb.at[n, pl.ds(2 * wave, 2)], xr.at[from_d, pl.ds(3 + 2 * wave, 2)]
        return remote(src, dst, on_send, x_recv.at[wave], pos, core)

    total = jnp.zeros((64, RANK), jnp.float32)
    for k in TIES + EARLY + LATE + [0]:
        d = other_d(k)
        rows = [xt[pl.ds(at(d // NX, zz, d % NX), 32, stride=128), :] for zz in range(NZ)]
        for zz in range(NZ):
            msg[d, pl.ds(lax.rem(zz + 2 * NZ - 2 - my_z, NZ), 1)] = rows[zz].reshape(1, 32, 128)
        if k in TIES:
            via_copy(TIES.index(k)).start()
        if k in EARLY:
            x_copy(k, 0).start()
            x_copy(k, 1).start()
        xb = jnp.concatenate(rows, axis=0).T.astype(jnp.bfloat16)
        low = sv[d // NX, :, d % NX, 0:32, :].reshape(256, RANK)
        high = sv[d // NX, :, d % NX, 32:64, :].reshape(256, RANK)
        total = total + nn(xb[0:64], low) + nn(xb[64:128], high)
    part[...] = total
    pair = remote(part, other, pair_send, pair_recv, me, sibling)
    pair.start()
    xr[pl.ds(my_d, 1)] = msg[pl.ds(my_d, 1)]
    pair.wait()
    yl[...] = part[...] + other[...]
    my_half = pl.ds(pl.multiple_of(core * 32, 32), 32)
    yp[pl.ds(core, 1), pl.ds(my_d, 1)] = yl[my_half, :].reshape(1, 1, 32, RANK)
    gl[...] = tn(yl[...], yl[...], HIGHEST)

    def g_copy(k):
        d = other_d(k)
        rows = pl.ds(pl.multiple_of(core * 128 + d * 8, 8), 8)
        return remote(gl.at[rows, :], gr.at[my_d], g_send, g_recv, at_d(d), core)

    def gz_copy(k):
        z = other_z(k)
        return remote(gp, gz.at[my_z], gz_send, gz_recv, at(my_y, z, my_x), core)

    my_rows = pl.ds(pl.multiple_of((core * PLANE + my_d) * 8, 8), 8)

    def gf_copy(d, q):
        return remote(gf, gm.at[my_rows, :], gf_send, gf_recv, at_d(d), q)

    def y_copy(k):
        d = other_d(k)
        return remote(yl.at[my_half, :], yp.at[core, my_d], y_send, y_recv, at_d(d), core)

    half_copy = remote(yp.at[core], yp.at[core], half_send, half_recv, me, sibling)

    def own_copy(q):
        return pltpu.make_async_copy(yp.at[q], ya.at[0, q], own_sem.at[q])

    above, below = at(my_y, other_z(1), my_x), at(my_y, other_z(NZ - 1), my_x)

    def up_copy(r):
        src = yp.at[0] if r == 0 else ya.at[NZ - r, 0]
        dst = ya.at[NZ - 1 - r, 0]
        if r == 3:
            src, dst = src.at[pl.ds(0, 8)], dst.at[pl.ds(0, 8)]
        return remote(src, dst, up_send.at[r], up_recv.at[r], above, 0)

    def down_copy(r):
        src = yp.at[0] if r == 0 else ya.at[r, 0]
        dst = ya.at[1 + r, 0]
        if r == 3:
            src, dst = src.at[pl.ds(8, 8)], dst.at[pl.ds(8, 8)]
        return remote(src, dst, down_send.at[r], down_recv.at[r], below, 0)

    def forward(ref):
        remote(ref, ref, fwd_send, fwd_recv, me, sibling).start()

    def zd_copy(k):
        return remote(
            yl.at[my_half, :], ya.at[NZ - k, 1, my_d], zd_send, zd_recv, at(my_y, other_z(k), my_x), 1
        )

    near, far = pl.ds(1, 4), pl.ds(5, 3)

    upper, lower = pl.ds(0, 16), pl.ds(16, 16)

    def x_next(i):
        return lax.rem(my_x + i, NX)

    def y_next(i):
        return lax.rem(my_y + i, NY)

    def p1_copies(t):
        copies = []
        for q, (rel, block, along) in enumerate((
            (near, lambda i: my_y * NX + x_next(i), lambda i: at(my_y, my_z, x_next(i))),
            (far, lambda i: y_next(i) * NX + my_x, lambda i: at(y_next(i), my_z, my_x)),
        )):
            if t == 0:
                up, down = ya.at[rel, 1, block(0)], ya.at[rel, 1, block(0)]
            else:
                up, down = ya.at[rel, 1, block(3), upper], ya.at[rel, 1, block(1), lower]
            copies.append(remote(up, up, p1_send.at[t, q], p1_recv.at[t, q], along(1), 1))
            copies.append(remote(down, down, p1_send.at[t, q], p1_recv.at[t, q], along(3), 1))
        return copies

    def p2_copies(t):
        def row(i):
            return pl.ds(pl.multiple_of(y_next(i) * NX, NX), NX)

        copies = []
        if t == 0:
            up, down = ya.at[near, 1, row(0)], ya.at[near, 1, row(0)]
        else:
            up, down = ya.at[near, 1, row(3), upper], ya.at[near, 1, row(1), lower]
        copies.append(remote(up, up, p2_send.at[t, 0], p2_recv.at[t, 0], at(y_next(1), my_z, my_x), 1))
        copies.append(remote(down, down, p2_send.at[t, 0], p2_recv.at[t, 0], at(y_next(3), my_z, my_x), 1))
        for v in range(NY):
            if t == 0:
                up, down = ya.at[far, 1, v * NX + my_x], ya.at[far, 1, v * NX + my_x]
            else:
                up, down = ya.at[far, 1, v * NX + x_next(3), upper], ya.at[far, 1, v * NX + x_next(1), lower]
            copies.append(remote(up, up, p2_send.at[t, 1], p2_recv.at[t, 1], at(my_y, my_z, x_next(1)), 1))
            copies.append(remote(down, down, p2_send.at[t, 1], p2_recv.at[t, 1], at(my_y, my_z, x_next(3)), 1))
        return copies

    def p_forward(i):
        forward(ya.at[near, 1, pl.ds(pl.multiple_of(y_next(i) * NX, NX), NX)])
        for v in range(NY):
            forward(ya.at[far, 1, v * NX + x_next(i)])

    def p_size(phase, t):
        blocks = (1 if phase == 1 else 4) * (2 if t == 0 else 1)
        return [ya.at[near, 1, pl.ds(0, blocks)], ya.at[far, 1, pl.ds(0, blocks)]]

    def p_landed(phase, t):
        for q in range(2):
            landed(p_size(phase, t)[q], (p1_recv if phase == 1 else p2_recv).at[t, q])

    def p_start(phase, t):
        for copy in (p1_copies if phase == 1 else p2_copies)(t):
            copy.start()

    @pl.loop(1, PLANE)
    def _(k):
        g_copy(k).start()

    @pl.loop(1, PLANE)
    def _(k):
        y_copy(k).start()

    gr[pl.ds(my_d, 1)] = gl[my_rows, :].reshape(1, 8, RANK)

    @pl.when(core == 1)
    def _():
        @pl.loop(1, NZ)
        def _(k):
            zd_copy(k).start()

    landed(gr.at[pl.ds(0, PLANE - 1)], g_recv)
    gp[...] = jnp.sum(gr[...], axis=0)

    @pl.loop(1, NZ)
    def _(k):
        gz_copy(k).start()

    for k in LATE:
        x_copy(k, 0).start()
    gz[pl.ds(my_z, 1)] = gp[...].reshape(1, 8, RANK)
    landed(gz.at[pl.ds(0, NZ - 1)], gz_recv)
    gf[...] = jnp.sum(gz[...], axis=0)

    @pl.when(core == 0)
    def _():
        gf_copy(my_d, 1).start()

    @pl.loop(1, PLANE)
    def _(k):
        gf_copy(other_d(k), 1).start()

    gm[my_rows, :] = gf[...]
    landed(yp.at[core, pl.ds(0, PLANE - 1)], y_recv)
    half_copy.start()
    own_copy(core).start()

    @pl.when(core == 0)
    def _():
        up_copy(0).start()
        down_copy(0).start()

    @pl.when(core == 1)
    def _():
        landed(ya.at[pl.ds(1, NZ - 1), 1, my_d], zd_recv)
        p_start(1, 0)

    def frames_on(wave):
        if wave == 1:
            for k in LATE:
                x_copy(k, wave).start()
        for n in range(len(TIES)):
            if wave == 0:
                landed(vb.at[n], via_recv.at[n])
            on_copy(n, wave).start()
        for k in TIES:
            x_copy(k, wave).start()

    def ring_landed(r):
        if r < 3:
            landed(ya.at[NZ - 1 - r, 0], up_recv.at[r])
            landed(ya.at[1 + r, 0], down_recv.at[r])
        else:
            landed(ya.at[4, 0, pl.ds(0, 8)], up_recv.at[r])
            landed(ya.at[4, 0, pl.ds(8, 8)], down_recv.at[r])

    def ring_round(r):
        ring_landed(r - 1)
        up_copy(r).start()
        down_copy(r).start()
        forward(ya.at[NZ - r, 0])
        forward(ya.at[r, 0])

    def c_block(s, way):
        return pl.ds((2 - s if way == 0 else 2 + s) % NZ if s < 3 else (7 if way == 0 else 5), 1)

    def c_rows(s, way):
        return pl.ds(0, 32) if s else pl.ds(16 * way, 16)

    def c_copy(s, way):
        src, dst = cacc.at[c_block(s, way), c_rows(s, way)], cr.at[way, pl.ds(s, 1), c_rows(s, way)]
        return remote(src, dst, c_send.at[way, s], c_recv.at[way, s], above if way == 0 else below, core)

    def c_landed(s, way):
        landed(cr.at[way, pl.ds(s, 1), c_rows(s, way)], c_recv.at[way, s])

    def c_step(s):
        for way in range(2):
            if s:
                c_landed(s - 1, way)
                rows = c_rows(s - 1, way)
                cacc[c_block(s, way), rows] += cr[way, pl.ds(s - 1, 1), rows]
            c_copy(s, way).start()

    def coefficients(rows):
        ks = range(PLANE)
        total = jnp.zeros((rows.size * 32, 2 * RANK), jnp.float32)
        zero = jnp.zeros((64, RANK), jnp.float32)
        for n in range(0, len(ks), 2):
            lhs, rhs = [], []
            for k in ks[n : n + 2]:
                d = other_d(k)
                y = jnp.concatenate([yp[0, d], yp[1, d]], axis=0)
                lhs.append(xr[d, rows].reshape(rows.size * 32, 128))
                rhs.append(jnp.concatenate([y, zero], axis=1))
                rhs.append(jnp.concatenate([zero, y], axis=1))
            ah, al = halves(jnp.concatenate(lhs, axis=1))
            bh, bl = halves(jnp.concatenate(rhs, axis=0))
            total = total + (nn(ah, bh) + nn(ah, bl) + nn(al, bh))
        cacc[rows] = total.reshape(rows.size, 32, 2 * RANK)

    def first_sums():
        landed(yp.at[sibling], half_recv)
        own_copy(sibling).start()
        landed(xr.at[pl.ds(0, PLANE - 1), pl.ds(0, 5)], x_recv.at[0])
        coefficients(pl.ds(0, 5))
        c_step(0)

    def second_sums():
        landed(xr.at[pl.ds(0, PLANE - 1), pl.ds(0, 3)], x_recv.at[1])
        coefficients(pl.ds(5, 3))
        c_step(3)

    def step(o, last):
        @pl.when(o == 1)
        def _():
            p_landed(1, 1)
            p_start(2, 0)
            frames_on(1)
            p_forward(0)

        @pl.when(o == 4)
        def _():
            first_sums()

        @pl.when(o == 6)
        def _():
            c_step(1)
            p_landed(2, 0)
            p_start(2, 1)
            p_forward(1)
            p_forward(3)

        @pl.when(o == 7)
        def _():
            c_step(2)

        return factor_step(o, last, gm)

    @pl.when(core == 0)
    def _():
        frames_on(0)
        frames_on(1)
        ring_round(1)
        first_sums()
        ring_round(2)
        c_step(1)
        c_step(2)
        second_sums()
        ring_round(3)
        landed(gi, gi_recv)

    gi_copy = remote(gi, gi, gi_send, gi_recv, me, 0)

    @pl.when(core == 1)
    def _():
        p_landed(1, 0)
        p_start(1, 1)
        frames_on(0)
        landed(gm.at[pl.ds(0, RANK - 8), :], gf_recv)
        panels = RANK // PANEL
        gm[RANK - PANEL : RANK, :] = lax.fori_loop(0, panels, step, jnp.zeros((PANEL, RANK), jnp.float32))
        row_at = lax.broadcasted_iota(jnp.int32, (RANK, RANK), 0)
        lane_at = lax.broadcasted_iota(jnp.int32, (RANK, RANK), 1)
        factor = jnp.where(lane_at <= row_at, gm[...], 0.0)
        gi[...] = tn(factor, factor, HIGHEST)
        gi_copy.start()
        second_sums()

    c_landed(3, 0)
    c_landed(3, 1)
    c = cacc[6] + (cr[0, 3] + cr[1, 3])
    c = jnp.concatenate([c[:, 0:RANK], c[:, RANK:]], axis=0)
    w_ref[...] = nn(c, gi[...], HIGHEST)

    @pl.when(core == 0)
    def _():
        ring_landed(3)
        forward(ya.at[4, 0])

    @pl.when(core == 1)
    def _():
        p_landed(2, 1)
        p_forward(2)

    landed(ya.at[pl.ds(1, NZ - 1), sibling], fwd_recv)
    left(ya.at[pl.ds(1, NZ - 1), core], fwd_send)
    left(gz.at[pl.ds(0, NZ - 1)], gz_send)
    for s in range(4):
        c_copy(s, 0).wait_send()
        c_copy(s, 1).wait_send()
    left(yp.at[core], half_send)
    own_copy(0).wait()
    own_copy(1).wait()
    left(gr.at[pl.ds(0, PLANE - 1)], gf_send)
    left(gr.at[pl.ds(0, PLANE - 1)], g_send)
    left(yp.at[core, pl.ds(0, PLANE - 1)], y_send)
    left(vb, via_send)
    left(vb, on_send)
    left(xr.at[pl.ds(0, len(EARLY + LATE))], x_send)
    left(vb, x_send)

    @pl.when(core == 0)
    def _():
        gf_copy(my_d, 1).wait_send()
        for r in range(4):
            up_copy(r).wait_send()
            down_copy(r).wait_send()

    @pl.when(core == 1)
    def _():
        gi_copy.wait_send()
        left(ya.at[pl.ds(1, NZ - 1), 1, my_d], zd_send)
        for t in range(2):
            for q in range(2):
                left(p_size(1, t)[q], p1_send.at[t, q])
                left(p_size(2, t)[q], p2_send.at[t, q])


def rebuild_kernel(w_ref, y_ref, out_ref):
    my_z = (lax.axis_index("pos") // NX) % NZ
    wh, wl = halves(w_ref[...])
    both = jnp.concatenate([wh, wl], axis=0)
    for rel in range(NZ):
        yh, yl = halves(jnp.concatenate([y_ref[rel, q, x] for x in range(NX) for q in range(2)], axis=0))
        two = nt(both, yh)
        z = lax.rem(my_z + rel, NZ)
        lanes = pl.ds(pl.multiple_of(z * 64 * NX, 64 * NX), 64 * NX)
        out_ref[0, :, lanes] = two[0:64] + (two[64:128] + nt(wh, yl))


VMEM = pl.BlockSpec(memory_space=pltpu.VMEM)
ANY = pl.BlockSpec(memory_space=pl.ANY)
DMA = pltpu.SemaphoreType.DMA


def body(frames, sketch):
    x = frames.transpose(0, 2, 1).reshape(64 * 64, 128)
    s = sketch.reshape(NY, NZ, NX, 64, RANK)
    f32 = jnp.float32
    w, y_all = pl.pallas_call(
        main_kernel,
        out_shape=[
            jax.ShapeDtypeStruct((64, RANK), f32),
            jax.ShapeDtypeStruct((NZ, 2, PLANE, 32, RANK), f32),
        ],
        in_specs=[ANY, ANY],
        out_specs=[VMEM, ANY],
        scratch_shapes=[
            pltpu.VMEM((4096, 128), f32),
            pltpu.VMEM((4096, 128), f32),
            pltpu.VMEM((NY, NZ, NX, 64, RANK), jnp.bfloat16),
            pltpu.VMEM((PLANE, NZ, 32, 128), f32),
            pltpu.VMEM((PLANE, NZ, 32, 128), f32),
            pltpu.VMEM((64, RANK), f32),
            pltpu.VMEM((64, RANK), f32),
            pltpu.VMEM((64, RANK), f32),
            pltpu.VMEM((2, PLANE, 32, RANK), f32),
            pltpu.VMEM((RANK, RANK), f32),
            pltpu.VMEM((PLANE, 8, RANK), f32),
            pltpu.VMEM((8, RANK), f32),
            pltpu.VMEM((NZ, 8, RANK), f32),
            pltpu.VMEM((8, RANK), f32),
            pltpu.VMEM((RANK, RANK), f32),
            pltpu.VMEM((NZ, 32, 2 * RANK), f32),
            pltpu.VMEM((2, 4, 32, 2 * RANK), f32),
            pltpu.VMEM((len(TIES), 4, 32, 128), f32),
            pltpu.VMEM((RANK, RANK), f32),
            DMA, DMA, DMA, DMA,
            DMA, DMA((2,)), DMA, DMA, DMA, DMA, DMA((2,)),
            DMA, DMA, DMA, DMA, DMA, DMA, DMA((2, 4)), DMA((2, 4)),
            DMA((4,)), DMA((4,)), DMA((4,)), DMA((4,)),
            DMA, DMA, DMA((2, 2)), DMA((2, 2)), DMA((2, 2)), DMA((2, 2)), DMA, DMA,
            DMA, DMA((len(TIES),)), DMA, DMA, DMA,
        ],
        compiler_params=pltpu.CompilerParams(collective_id=0, has_side_effects=True, vmem_limit_bytes=58 << 20),
        cost_estimate=pl.CostEstimate(flops=4 * 10**9, bytes_accessed=3 * 10**7, transcendentals=0),
    )(x, s)
    y_all = y_all.reshape(NZ, 2, NY, NX, 32, RANK)
    return pl.pallas_call(
        rebuild_kernel,
        out_shape=jax.ShapeDtypeStruct((1, 64, 8192), f32),
        grid=(NY,),
        in_specs=[
            pl.BlockSpec((64, RANK), lambda i: (0, 0)),
            pl.BlockSpec((NZ, 2, None, NX, 32, RANK), lambda i: (0, 0, i, 0, 0, 0)),
        ],
        out_specs=pl.BlockSpec((1, 64, 2048), lambda i: (0, 0, i)),
        compiler_params=pltpu.CompilerParams(vmem_limit_bytes=58 << 20),
    )(w, y_all)


def solution(mesh):
    in_specs = (P("pos", None, "pix"), P(None, "pix", None))
    out_specs = P("pos", "pix", None)
    return jax.shard_map(body, mesh=mesh, in_specs=in_specs, out_specs=out_specs, check_vma=False)
```

```python
import jax
import jax.numpy as jnp
from jax import lax
from jax.experimental import pallas as pl
from jax.experimental.pallas import tpu as pltpu
from jax.sharding import PartitionSpec as P

MESH = pl.DeviceIdType.MESH
HIGHEST = lax.Precision.HIGHEST
NY, NZ, NX = 4, 8, 4
PLANE = NY * NX
RANK = 256
BLOCK, PANEL = 8, 32
TIES = [k for k in range(1, PLANE) if k // NX == 2 or k % NX == 2]
EARLY = [1, 3]
LATE = [k for k in range(1, PLANE) if k not in TIES + EARLY]


def tn(a, b, precision=None):
    return lax.dot_general(a, b, (((0,), (0,)), ((), ())), precision=precision, preferred_element_type=jnp.float32)


def nt(a, b, precision=None):
    return lax.dot_general(a, b, (((1,), (1,)), ((), ())), precision=precision, preferred_element_type=jnp.float32)


def nn(a, b, precision=None):
    return jnp.dot(a, b, precision=precision, preferred_element_type=jnp.float32)


def halves(a):
    high = a.astype(jnp.bfloat16)
    return high, (a - high.astype(jnp.float32)).astype(jnp.bfloat16)


def splat(rows, i):
    return jnp.broadcast_to(rows[:, i : i + 1], (BLOCK, 128))


def lanes_of(rows, base):
    tile = jnp.where(base < 128, rows[:, 0:128], rows[:, 128:256])
    return pltpu.roll(tile, lax.rem(256 - base, 128), 1)


def factor_diagonal(a):
    groups = [a[g * BLOCK : (g + 1) * BLOCK] for g in range(PANEL // BLOCK)]
    sub = lax.broadcasted_iota(jnp.int32, (BLOCK, 128), 0)
    for q in range(PANEL // BLOCK):
        rows = [jnp.broadcast_to(groups[q][k : k + 1, :], (BLOCK, 128)) for k in range(BLOCK)]
        columns = [[splat(groups[g], q * BLOCK + k) for k in range(BLOCK)] for g in range(q + 1, PANEL // BLOCK)]
        s = [[splat(rows[i], q * BLOCK + k) for k in range(i + 1)] for i in range(BLOCK)]
        inv, done = [], []
        for k in range(BLOCK):
            inv.append(lax.rsqrt(s[k][k]))
            for i in range(k + 1, BLOCK):
                s[i][k] = s[i][k] * inv[k]
            for i in range(k + 1, BLOCK):
                for m in range(k + 1, i + 1):
                    s[i][m] = s[i][m] - s[i][k] * s[m][k]
            row = rows[k]
            for i in range(k):
                row = row - s[k][i] * done[i]
            done.append(row * inv[k])
        for g in range(q + 1, PANEL // BLOCK):
            times = []
            for k in range(BLOCK):
                t = columns[g - q - 1][k]
                for i in range(k):
                    t = t - times[i] * s[k][i]
                times.append(t * inv[k])
                groups[g] = groups[g] - times[k] * done[k]
        block = done[0]
        for k in range(1, BLOCK):
            block = jnp.where(sub == k, done[k], block)
        groups[q] = block
    return jnp.concatenate(groups, axis=0)


def factor_step(o, last, a_ref):
    base = pl.multiple_of(o * PANEL, PANEL)
    lane = lax.broadcasted_iota(jnp.int32, (1, RANK), 1)
    before = (lane >= base - PANEL) & (lane < base)
    rows = jnp.where(before, 0.0, a_ref[pl.ds(base, PANEL), :])
    rows = rows - tn(lanes_of(last, base)[:, 0:PANEL], last, HIGHEST)
    row_at = lax.broadcasted_iota(jnp.int32, (PANEL, 128), 0)
    lane_at = lax.broadcasted_iota(jnp.int32, (PANEL, 128), 1)
    both = jnp.where(lane_at < PANEL, lanes_of(rows, base), jnp.where(lane_at == row_at + PANEL, 1.0, 0.0))
    both = factor_diagonal(both)
    inverse = jnp.where((lane_at >= PANEL) & (lane_at < 2 * PANEL), both, 0.0)
    own = (lane >= base) & (lane < base + PANEL)
    unit = lane == base + lax.broadcasted_iota(jnp.int32, (PANEL, 1), 0)
    rows = jnp.where(own, jnp.where(unit, 1.0, 0.0), rows)
    zeros = jnp.zeros((PANEL, RANK), jnp.float32)
    panel = nn(inverse, jnp.concatenate([zeros, rows, zeros, zeros], axis=0), HIGHEST)
    right = jnp.where(lane >= base, last, 0.0)
    below = lax.broadcasted_iota(jnp.int32, (RANK, 1), 0) >= base
    a_ref[...] = jnp.where(below & before, 0.0, a_ref[...]) - tn(right, last, HIGHEST)

    @pl.when(o > 0)
    def _():
        a_ref[pl.ds(pl.multiple_of(jnp.maximum(base - PANEL, 0), PANEL), PANEL), :] = last

    return panel


def main_kernel(
    x_hbm, s_hbm, w_ref, ya,
    xv, xt, sv, msg, xr, part, other, yl, yp, gl, gr, gp, gz, gf, gm, cacc, cr, vb, gi,
    x_in, s_in, pair_send, pair_recv, x_send, x_recv, y_send, y_recv, half_send, half_recv, own_sem,
    g_send, g_recv, gz_send, gz_recv, gf_send, gf_recv, c_send, c_recv,
    up_send, up_recv, down_send, down_recv, zd_send, zd_recv, p1_send, p1_recv, p2_send, p2_recv, fwd_send, fwd_recv,
    via_send, via_recv, on_send, gi_send, gi_recv,
):
    me = lax.axis_index("pos")
    core = lax.axis_index("pix")
    my_y, my_z, my_x = me // (NZ * NX), (me // NX) % NZ, me % NX
    my_d = my_y * NX + my_x
    sibling = 1 - core

    def at(y, z, x):
        return y * (NZ * NX) + z * NX + x

    def at_d(d):
        return at(d // NX, my_z, d % NX)

    def other_d(k):
        return lax.rem(my_y + k // NX, NY) * NX + lax.rem(my_x + k % NX, NX)

    def other_z(k):
        return lax.rem(my_z + k, NZ)

    def remote(src, dst, send_sem, recv_sem, pos, to_core):
        return pltpu.make_async_remote_copy(
            src_ref=src, dst_ref=dst, send_sem=send_sem, recv_sem=recv_sem,
            device_id={"pos": pos, "pix": to_core}, device_id_type=MESH,
        )

    def landed(ref, sem):
        remote(ref, ref, own_sem.at[0], sem, me, sibling).wait_recv()

    def left(ref, sem):
        remote(ref, ref, sem, own_sem.at[0], me, sibling).wait_send()

    x_copy_in = pltpu.make_async_copy(x_hbm, xv, x_in)
    x_copy_in.start()
    s_copy_in = pltpu.make_async_copy(s_hbm, sv, s_in)
    s_copy_in.start()

    barrier = pltpu.get_barrier_semaphore()

    def greet(pos, to_core):
        pl.semaphore_signal(barrier, inc=1, device_id={"pos": pos, "pix": to_core}, device_id_type=MESH)

    greet(me, sibling)

    @pl.loop(1, PLANE)
    def _(k):
        greet(at_d(other_d(k)), core)
        greet(at_d(other_d(k)), sibling)

    @pl.loop(1, NZ)
    def _(k):
        greet(at(my_y, other_z(k), my_x), core)

    x_copy_in.wait()

    @pl.loop(0, 32, unroll=4)
    def _(cp):
        low = xv[pl.ds(cp, 64, stride=64), :]
        high = xv[pl.ds(cp + 32, 64, stride=64), :]
        xt[pl.ds(pl.multiple_of(cp * 128, 128), 128), :] = jnp.concatenate([low, high], axis=0).T

    s_copy_in.wait()
    pl.semaphore_wait(barrier, 1 + 2 * (PLANE - 1) + NZ - 1)

    def x_copy(k, wave):
        d = other_d(k)
        if k in TIES:
            rows = pl.ds(0, 3) if wave == 0 else pl.ds(7, 1)
        else:
            rows = pl.ds(0, 5) if wave == 0 else pl.ds(5, 3)
        return remote(msg.at[d, rows], xr.at[my_d, rows], x_send, x_recv.at[wave], at_d(d), core)

    def via(k):
        return 3 if k // NX == 2 else k // NX, 3 if k % NX == 2 else k % NX

    def via_copy(n):
        k = TIES[n]
        vy, vx = via(k)
        pos = at(lax.rem(my_y + vy, NY), my_z, lax.rem(my_x + vx, NX))
        return remote(msg.at[other_d(k), pl.ds(3, 4)], vb.at[n], via_send, via_recv.at[n], pos, core)

    def on_copy(n, wave):
        k = TIES[n]
        vy, vx = via(k)
        from_d = lax.rem(my_y + NY - vy, NY) * NX + lax.rem(my_x + NX - vx, NX)
        pos = at(lax.rem(my_y + NY + k // NX - vy, NY), my_z, lax.rem(my_x + NX + k % NX - vx, NX))
        src, dst = vb.at[n, pl.ds(2 * wave, 2)], xr.at[from_d, pl.ds(3 + 2 * wave, 2)]
        return remote(src, dst, on_send, x_recv.at[wave], pos, core)

    total = jnp.zeros((64, RANK), jnp.float32)
    for k in TIES + EARLY + LATE + [0]:
        d = other_d(k)
        rows = [xt[pl.ds(at(d // NX, zz, d % NX), 32, stride=128), :] for zz in range(NZ)]
        for zz in range(NZ):
            msg[d, pl.ds(lax.rem(zz + 2 * NZ - 2 - my_z, NZ), 1)] = rows[zz].reshape(1, 32, 128)
        if k in TIES:
            via_copy(TIES.index(k)).start()
        if k in EARLY:
            x_copy(k, 0).start()
            x_copy(k, 1).start()
        xb = jnp.concatenate(rows, axis=0).T.astype(jnp.bfloat16)
        low = sv[d // NX, :, d % NX, 0:32, :].reshape(256, RANK)
        high = sv[d // NX, :, d % NX, 32:64, :].reshape(256, RANK)
        total = total + nn(xb[0:64], low) + nn(xb[64:128], high)
    part[...] = total
    pair = remote(part, other, pair_send, pair_recv, me, sibling)
    pair.start()
    xr[pl.ds(my_d, 1)] = msg[pl.ds(my_d, 1)]
    pair.wait()
    yl[...] = part[...] + other[...]
    my_half = pl.ds(pl.multiple_of(core * 32, 32), 32)
    yp[pl.ds(core, 1), pl.ds(my_d, 1)] = yl[my_half, :].reshape(1, 1, 32, RANK)
    gl[...] = tn(yl[...], yl[...], HIGHEST)

    def g_copy(k):
        d = other_d(k)
        rows = pl.ds(pl.multiple_of(core * 128 + d * 8, 8), 8)
        return remote(gl.at[rows, :], gr.at[my_d], g_send, g_recv, at_d(d), core)

    def gz_copy(k):
        z = other_z(k)
        return remote(gp, gz.at[my_z], gz_send, gz_recv, at(my_y, z, my_x), core)

    my_rows = pl.ds(pl.multiple_of((core * PLANE + my_d) * 8, 8), 8)

    def gf_copy(d, q):
        return remote(gf, gm.at[my_rows, :], gf_send, gf_recv, at_d(d), q)

    def y_copy(k):
        d = other_d(k)
        return remote(yl.at[my_half, :], yp.at[core, my_d], y_send, y_recv, at_d(d), core)

    half_copy = remote(yp.at[core], yp.at[core], half_send, half_recv, me, sibling)

    def own_copy(q):
        return pltpu.make_async_copy(yp.at[q], ya.at[0, q], own_sem.at[q])

    above, below = at(my_y, other_z(1), my_x), at(my_y, other_z(NZ - 1), my_x)

    def up_copy(r):
        src = yp.at[0] if r == 0 else ya.at[NZ - r, 0]
        dst = ya.at[NZ - 1 - r, 0]
        if r == 3:
            src, dst = src.at[pl.ds(0, 8)], dst.at[pl.ds(0, 8)]
        return remote(src, dst, up_send.at[r], up_recv.at[r], above, 0)

    def down_copy(r):
        src = yp.at[0] if r == 0 else ya.at[r, 0]
        dst = ya.at[1 + r, 0]
        if r == 3:
            src, dst = src.at[pl.ds(8, 8)], dst.at[pl.ds(8, 8)]
        return remote(src, dst, down_send.at[r], down_recv.at[r], below, 0)

    def forward(ref):
        remote(ref, ref, fwd_send, fwd_recv, me, sibling).start()

    def zd_copy(k):
        return remote(
            yl.at[my_half, :], ya.at[NZ - k, 1, my_d], zd_send, zd_recv, at(my_y, other_z(k), my_x), 1
        )

    near, far = pl.ds(1, 4), pl.ds(5, 3)

    upper, lower = pl.ds(0, 16), pl.ds(16, 16)

    def x_next(i):
        return lax.rem(my_x + i, NX)

    def y_next(i):
        return lax.rem(my_y + i, NY)

    def p1_copies(t):
        copies = []
        for q, (rel, block, along) in enumerate((
            (near, lambda i: my_y * NX + x_next(i), lambda i: at(my_y, my_z, x_next(i))),
            (far, lambda i: y_next(i) * NX + my_x, lambda i: at(y_next(i), my_z, my_x)),
        )):
            if t == 0:
                up, down = ya.at[rel, 1, block(0)], ya.at[rel, 1, block(0)]
            else:
                up, down = ya.at[rel, 1, block(3), upper], ya.at[rel, 1, block(1), lower]
            copies.append(remote(up, up, p1_send.at[t, q], p1_recv.at[t, q], along(1), 1))
            copies.append(remote(down, down, p1_send.at[t, q], p1_recv.at[t, q], along(3), 1))
        return copies

    def p2_copies(t):
        def row(i):
            return pl.ds(pl.multiple_of(y_next(i) * NX, NX), NX)

        copies = []
        if t == 0:
            up, down = ya.at[near, 1, row(0)], ya.at[near, 1, row(0)]
        else:
            up, down = ya.at[near, 1, row(3), upper], ya.at[near, 1, row(1), lower]
        copies.append(remote(up, up, p2_send.at[t, 0], p2_recv.at[t, 0], at(y_next(1), my_z, my_x), 1))
        copies.append(remote(down, down, p2_send.at[t, 0], p2_recv.at[t, 0], at(y_next(3), my_z, my_x), 1))
        for v in range(NY):
            if t == 0:
                up, down = ya.at[far, 1, v * NX + my_x], ya.at[far, 1, v * NX + my_x]
            else:
                up, down = ya.at[far, 1, v * NX + x_next(3), upper], ya.at[far, 1, v * NX + x_next(1), lower]
            copies.append(remote(up, up, p2_send.at[t, 1], p2_recv.at[t, 1], at(my_y, my_z, x_next(1)), 1))
            copies.append(remote(down, down, p2_send.at[t, 1], p2_recv.at[t, 1], at(my_y, my_z, x_next(3)), 1))
        return copies

    def p_forward(i):
        forward(ya.at[near, 1, pl.ds(pl.multiple_of(y_next(i) * NX, NX), NX)])
        for v in range(NY):
            forward(ya.at[far, 1, v * NX + x_next(i)])

    def p_size(phase, t):
        blocks = (1 if phase == 1 else 4) * (2 if t == 0 else 1)
        return [ya.at[near, 1, pl.ds(0, blocks)], ya.at[far, 1, pl.ds(0, blocks)]]

    def p_landed(phase, t):
        for q in range(2):
            landed(p_size(phase, t)[q], (p1_recv if phase == 1 else p2_recv).at[t, q])

    def p_start(phase, t):
        for copy in (p1_copies if phase == 1 else p2_copies)(t):
            copy.start()

    @pl.loop(1, PLANE)
    def _(k):
        g_copy(k).start()

    @pl.loop(1, PLANE)
    def _(k):
        y_copy(k).start()

    for k in LATE:
        x_copy(k, 0).start()
    gr[pl.ds(my_d, 1)] = gl[my_rows, :].reshape(1, 8, RANK)

    @pl.when(core == 1)
    def _():
        @pl.loop(1, NZ)
        def _(k):
            zd_copy(k).start()

    landed(gr.at[pl.ds(0, PLANE - 1)], g_recv)
    gp[...] = jnp.sum(gr[...], axis=0)

    @pl.loop(1, NZ)
    def _(k):
        gz_copy(k).start()

    gz[pl.ds(my_z, 1)] = gp[...].reshape(1, 8, RANK)
    landed(gz.at[pl.ds(0, NZ - 1)], gz_recv)
    gf[...] = jnp.sum(gz[...], axis=0)

    @pl.when(core == 0)
    def _():
        gf_copy(my_d, 1).start()

    @pl.loop(1, PLANE)
    def _(k):
        gf_copy(other_d(k), 1).start()

    gm[my_rows, :] = gf[...]
    landed(yp.at[core, pl.ds(0, PLANE - 1)], y_recv)
    half_copy.start()
    own_copy(core).start()

    @pl.when(core == 0)
    def _():
        up_copy(0).start()
        down_copy(0).start()

    @pl.when(core == 1)
    def _():
        landed(ya.at[pl.ds(1, NZ - 1), 1, my_d], zd_recv)
        p_start(1, 0)

    def frames_on(wave):
        if wave == 1:
            for k in LATE:
                x_copy(k, wave).start()
        for n in range(len(TIES)):
            if wave == 0:
                landed(vb.at[n], via_recv.at[n])
            on_copy(n, wave).start()
        for k in TIES:
            x_copy(k, wave).start()

    def ring_landed(r):
        if r < 3:
            landed(ya.at[NZ - 1 - r, 0], up_recv.at[r])
            landed(ya.at[1 + r, 0], down_recv.at[r])
        else:
            landed(ya.at[4, 0, pl.ds(0, 8)], up_recv.at[r])
            landed(ya.at[4, 0, pl.ds(8, 8)], down_recv.at[r])

    def ring_round(r):
        ring_landed(r - 1)
        up_copy(r).start()
        down_copy(r).start()
        forward(ya.at[NZ - r, 0])
        forward(ya.at[r, 0])

    def c_block(s, way):
        return pl.ds((2 - s if way == 0 else 2 + s) % NZ if s < 3 else (7 if way == 0 else 5), 1)

    def c_rows(s, way):
        return pl.ds(0, 32) if s else pl.ds(16 * way, 16)

    def c_copy(s, way):
        src, dst = cacc.at[c_block(s, way), c_rows(s, way)], cr.at[way, pl.ds(s, 1), c_rows(s, way)]
        return remote(src, dst, c_send.at[way, s], c_recv.at[way, s], above if way == 0 else below, core)

    def c_landed(s, way):
        landed(cr.at[way, pl.ds(s, 1), c_rows(s, way)], c_recv.at[way, s])

    def c_step(s):
        for way in range(2):
            if s:
                c_landed(s - 1, way)
                rows = c_rows(s - 1, way)
                cacc[c_block(s, way), rows] += cr[way, pl.ds(s - 1, 1), rows]
            c_copy(s, way).start()

    def coefficients(rows):
        ks = range(PLANE)
        total = jnp.zeros((rows.size * 32, 2 * RANK), jnp.float32)
        zero = jnp.zeros((64, RANK), jnp.float32)
        for n in range(0, len(ks), 2):
            lhs, rhs = [], []
            for k in ks[n : n + 2]:
                d = other_d(k)
                y = jnp.concatenate([yp[0, d], yp[1, d]], axis=0)
                lhs.append(xr[d, rows].reshape(rows.size * 32, 128))
                rhs.append(jnp.concatenate([y, zero], axis=1))
                rhs.append(jnp.concatenate([zero, y], axis=1))
            ah, al = halves(jnp.concatenate(lhs, axis=1))
            bh, bl = halves(jnp.concatenate(rhs, axis=0))
            total = total + (nn(ah, bh) + nn(ah, bl) + nn(al, bh))
        cacc[rows] = total.reshape(rows.size, 32, 2 * RANK)

    def first_sums():
        landed(yp.at[sibling], half_recv)
        own_copy(sibling).start()
        landed(xr.at[pl.ds(0, PLANE - 1), pl.ds(0, 5)], x_recv.at[0])
        coefficients(pl.ds(0, 5))
        c_step(0)

    def second_sums():
        landed(xr.at[pl.ds(0, PLANE - 1), pl.ds(0, 3)], x_recv.at[1])
        coefficients(pl.ds(5, 3))
        c_step(3)

    def step(o, last):
        @pl.when(o == 1)
        def _():
            p_landed(1, 1)
            p_start(2, 0)
            frames_on(1)
            p_forward(0)

        @pl.when(o == 4)
        def _():
            first_sums()

        @pl.when(o == 6)
        def _():
            c_step(1)

        @pl.when(o == 7)
        def _():
            c_step(2)

        return factor_step(o, last, gm)

    @pl.when(core == 0)
    def _():
        frames_on(0)
        frames_on(1)
        ring_round(1)
        first_sums()
        ring_round(2)
        c_step(1)
        c_step(2)
        second_sums()
        ring_round(3)
        landed(gi, gi_recv)

    gi_copy = remote(gi, gi, gi_send, gi_recv, me, 0)

    @pl.when(core == 1)
    def _():
        p_landed(1, 0)
        p_start(1, 1)
        frames_on(0)
        landed(gm.at[pl.ds(0, RANK - 8), :], gf_recv)
        panels = RANK // PANEL
        gm[RANK - PANEL : RANK, :] = lax.fori_loop(0, panels, step, jnp.zeros((PANEL, RANK), jnp.float32))
        row_at = lax.broadcasted_iota(jnp.int32, (RANK, RANK), 0)
        lane_at = lax.broadcasted_iota(jnp.int32, (RANK, RANK), 1)
        factor = jnp.where(lane_at <= row_at, gm[...], 0.0)
        gi[...] = tn(factor, factor, HIGHEST)
        gi_copy.start()
        p_landed(2, 0)
        p_start(2, 1)
        p_forward(1)
        p_forward(3)
        second_sums()

    c_landed(3, 0)
    c_landed(3, 1)
    c = cacc[6] + (cr[0, 3] + cr[1, 3])
    c = jnp.concatenate([c[:, 0:RANK], c[:, RANK:]], axis=0)
    w_ref[...] = nn(c, gi[...], HIGHEST)

    @pl.when(core == 0)
    def _():
        ring_landed(3)
        forward(ya.at[4, 0])

    @pl.when(core == 1)
    def _():
        p_landed(2, 1)
        p_forward(2)

    landed(ya.at[pl.ds(1, NZ - 1), sibling], fwd_recv)
    left(ya.at[pl.ds(1, NZ - 1), core], fwd_send)
    left(gz.at[pl.ds(0, NZ - 1)], gz_send)
    for s in range(4):
        c_copy(s, 0).wait_send()
        c_copy(s, 1).wait_send()
    left(yp.at[core], half_send)
    own_copy(0).wait()
    own_copy(1).wait()
    left(gr.at[pl.ds(0, PLANE - 1)], gf_send)
    left(gr.at[pl.ds(0, PLANE - 1)], g_send)
    left(yp.at[core, pl.ds(0, PLANE - 1)], y_send)
    left(vb, via_send)
    left(vb, on_send)
    left(xr.at[pl.ds(0, len(EARLY + LATE))], x_send)
    left(vb, x_send)

    @pl.when(core == 0)
    def _():
        gf_copy(my_d, 1).wait_send()
        for r in range(4):
            up_copy(r).wait_send()
            down_copy(r).wait_send()

    @pl.when(core == 1)
    def _():
        gi_copy.wait_send()
        left(ya.at[pl.ds(1, NZ - 1), 1, my_d], zd_send)
        for t in range(2):
            for q in range(2):
                left(p_size(1, t)[q], p1_send.at[t, q])
                left(p_size(2, t)[q], p2_send.at[t, q])


def rebuild_kernel(w_ref, y_ref, out_ref):
    my_z = (lax.axis_index("pos") // NX) % NZ
    wh, wl = halves(w_ref[...])
    both = jnp.concatenate([wh, wl], axis=0)
    for rel in range(NZ):
        yh, yl = halves(jnp.concatenate([y_ref[rel, q, x] for x in range(NX) for q in range(2)], axis=0))
        two = nt(both, yh)
        z = lax.rem(my_z + rel, NZ)
        lanes = pl.ds(pl.multiple_of(z * 64 * NX, 64 * NX), 64 * NX)
        out_ref[0, :, lanes] = two[0:64] + (two[64:128] + nt(wh, yl))


VMEM = pl.BlockSpec(memory_space=pltpu.VMEM)
ANY = pl.BlockSpec(memory_space=pl.ANY)
DMA = pltpu.SemaphoreType.DMA


def body(frames, sketch):
    x = frames.transpose(0, 2, 1).reshape(64 * 64, 128)
    s = sketch.reshape(NY, NZ, NX, 64, RANK)
    f32 = jnp.float32
    w, y_all = pl.pallas_call(
        main_kernel,
        out_shape=[
            jax.ShapeDtypeStruct((64, RANK), f32),
            jax.ShapeDtypeStruct((NZ, 2, PLANE, 32, RANK), f32),
        ],
        in_specs=[ANY, ANY],
        out_specs=[VMEM, ANY],
        scratch_shapes=[
            pltpu.VMEM((4096, 128), f32),
            pltpu.VMEM((4096, 128), f32),
            pltpu.VMEM((NY, NZ, NX, 64, RANK), jnp.bfloat16),
            pltpu.VMEM((PLANE, NZ, 32, 128), f32),
            pltpu.VMEM((PLANE, NZ, 32, 128), f32),
            pltpu.VMEM((64, RANK), f32),
            pltpu.VMEM((64, RANK), f32),
            pltpu.VMEM((64, RANK), f32),
            pltpu.VMEM((2, PLANE, 32, RANK), f32),
            pltpu.VMEM((RANK, RANK), f32),
            pltpu.VMEM((PLANE, 8, RANK), f32),
            pltpu.VMEM((8, RANK), f32),
            pltpu.VMEM((NZ, 8, RANK), f32),
            pltpu.VMEM((8, RANK), f32),
            pltpu.VMEM((RANK, RANK), f32),
            pltpu.VMEM((NZ, 32, 2 * RANK), f32),
            pltpu.VMEM((2, 4, 32, 2 * RANK), f32),
            pltpu.VMEM((len(TIES), 4, 32, 128), f32),
            pltpu.VMEM((RANK, RANK), f32),
            DMA, DMA, DMA, DMA,
            DMA, DMA((2,)), DMA, DMA, DMA, DMA, DMA((2,)),
            DMA, DMA, DMA, DMA, DMA, DMA, DMA((2, 4)), DMA((2, 4)),
            DMA((4,)), DMA((4,)), DMA((4,)), DMA((4,)),
            DMA, DMA, DMA((2, 2)), DMA((2, 2)), DMA((2, 2)), DMA((2, 2)), DMA, DMA,
            DMA, DMA((len(TIES),)), DMA, DMA, DMA,
        ],
        compiler_params=pltpu.CompilerParams(collective_id=0, has_side_effects=True, vmem_limit_bytes=58 << 20),
        cost_estimate=pl.CostEstimate(flops=4 * 10**9, bytes_accessed=3 * 10**7, transcendentals=0),
    )(x, s)
    y_all = y_all.reshape(NZ, 2, NY, NX, 32, RANK)
    return pl.pallas_call(
        rebuild_kernel,
        out_shape=jax.ShapeDtypeStruct((1, 64, 8192), f32),
        grid=(NY,),
        in_specs=[
            pl.BlockSpec((64, RANK), lambda i: (0, 0)),
            pl.BlockSpec((NZ, 2, None, NX, 32, RANK), lambda i: (0, 0, i, 0, 0, 0)),
        ],
        out_specs=pl.BlockSpec((1, 64, 2048), lambda i: (0, 0, i)),
        compiler_params=pltpu.CompilerParams(vmem_limit_bytes=58 << 20),
    )(w, y_all)


def solution(mesh):
    in_specs = (P("pos", None, "pix"), P(None, "pix", None))
    out_specs = P("pos", "pix", None)
    return jax.shard_map(body, mesh=mesh, in_specs=in_specs, out_specs=out_specs, check_vma=False)
```
